32 devices in a mesh: dp: 8 (over y, x, core), red: 4 (over z).
Axes of the slice: x: 2, y: 2, z: 4, core: 2. Of those that a mesh axis runs over, the one named last changes fastest.
Arguments:
- frames: bfloat16 [512, 48, 1536], P(('dp', 'red')), may hold values from -36 to 36
- cotangent: bfloat16 [512, 48, 1536], P(('dp', 'red')), may hold values from -6 to 6
- w_in: bfloat16 [1536, 3072], P('red'), may hold values from -0.15625 to 0.15625
- kernel: float32 [31, 1536], replicated, may hold values from -1 to 1
- gain: float32 [1536], replicated, may hold values from 0.25 to 1.75
- lengths: int32 [512], replicated, may hold values from 1 to 47, as said below
Outputs:
- module_output: bfloat16 [512, 48, 1536], P(('dp', 'red'))
- frame_gradient: bfloat16 [512, 48, 1536], P(('dp', 'red'))
- grad_w_in: float32 [1536, 3072], P('red')
- grad_kernel: float32 [31, 1536], replicated
- grad_gain: float32 [1536], replicated
The draws below stay inside these ranges and needn't reach their ends.
Inputs may be any that keep to these rules, and one draw needn't show every extreme that they name: The slots of each device, in order, form 8 groups of 2 slots. The q-th slot of group j on the device with dp index i and red index r and the q-th slot of group j on the device with dp index (2 j + 1 - i) mod 8 and the same red index have lengths that sum to exactly 48. The slots of dp index 0 all hold at least three quarters of 48 frames, rounded up.
All inputs are finite; a program needn't handle non-finite values.
Results may differ from the reference program's by a relative error of at most 0.0054.
Values may be sent and summed in bfloat16 or wider, within the bound.
No kernel may reach another device: no remote copies, remote signals or barrier semaphores. Data moves between devices by JAX's collectives and lax.ppermute only.
A program may use at most 128 MiB of HBM per device.

```python
import math
import jax
import jax.numpy as jnp
from jax import lax

D = 1536
K = 31
UTT_DEV = 16
MAXLEN = 48
UTTS = 512
N_DP = 8
N_RED = 4


def draw_frames(key, part):
    key_base, key_rows, key_cols = jax.random.split(key, 3)
    row_scales = jnp.exp(jax.random.uniform(key_rows, (UTTS, MAXLEN, 1), jnp.float32, math.log(0.3), math.log(3.0)))
    col_scales = jnp.exp(jax.random.uniform(key_cols, (D,), jnp.float32, math.log(0.3), math.log(3.0)))
    base_draw = jnp.clip(jax.random.normal(key_base, (UTTS, MAXLEN, D), jnp.float32), -4.0, 4.0)
    return (base_draw * row_scales * col_scales).astype(jnp.bfloat16)


def draw_lengths(key, part):
    per_peer = UTT_DEV // N_DP
    key_base, key_long = jax.random.split(jax.random.fold_in(key, 7))
    base_draw = jax.random.randint(key_base, (N_RED, N_DP, per_peer, N_DP), 1, MAXLEN)
    long_floor = (3 * MAXLEN + 3) // 4
    long_draw = jax.random.randint(key_long, (N_RED, N_DP, per_peer), long_floor, MAXLEN)
    long_draw = long_draw.at[:, 0, 0].set(MAXLEN - 1)
    source = jnp.arange(N_DP, dtype=jnp.int32)
    target = jnp.arange(N_DP, dtype=jnp.int32)
    partner = (2 * target[:, None] + 1 - source[None, :]) % N_DP
    lower = jnp.minimum(source[None, :], partner)
    lower_full = jnp.broadcast_to(lower[None, :, None, :], base_draw.shape)
    picked = jnp.take_along_axis(base_draw, lower_full, axis=3)
    chosen = jnp.where(lower_full == 0, long_draw[..., None], picked)
    length_grid = jnp.where(source[None, None, None, :] == lower_full, chosen, MAXLEN - chosen)
    return jnp.transpose(length_grid, (3, 0, 1, 2)).reshape(N_DP * N_RED * UTT_DEV).astype(jnp.int32)


def levels(rng, shape, shards, least, largest):
    level = 1.0
    for dim, blocks in shards:
        draws = jax.random.uniform(jax.random.fold_in(jax.random.fold_in(rng, 6), dim), (blocks,), jnp.float32, least / len(shards), largest / len(shards))
        level = level * jnp.repeat(jnp.exp(draws), shape[dim] // blocks).reshape((-1,) + (1,) * (len(shape) - 1 - dim))
    return level


def bell_draw(key, dims, scale, most, cuts=(), kind=jnp.bfloat16):
    result = scale * jax.random.normal(key, dims, jnp.float32)
    if cuts:
        result = result * levels(key, dims, cuts, -0.22, 0.18)
    return jnp.clip(result, -most, most).astype(kind)


def setup_inputs(seed: int = 0) -> dict:
    arg_keys = jax.random.split(jax.random.key(seed), 7)
    frames = draw_frames(jax.random.fold_in(arg_keys[6], 71), 0)
    cotangent = bell_draw(arg_keys[1], (UTTS, MAXLEN, D), 1.0, 6.0, ((0, 32),))
    w_in = bell_draw(arg_keys[2], (D, 2 * D), D ** -0.5, 0.15625, ((0, 4),))
    kernel = bell_draw(arg_keys[3], (K, D), K ** -0.5, 1.0, (), jnp.float32)
    gain = jnp.clip(1.0 + 0.15 * jax.random.normal(arg_keys[4], (D,), jnp.float32), 0.25, 1.75)
    lengths = draw_lengths(jax.random.fold_in(arg_keys[6], 71), 0)
    return dict(frames=frames, cotangent=cotangent, w_in=w_in, kernel=kernel, gain=gain, lengths=lengths)


EPSILON = 1e-05

def normalize(widened_frames):
    center = widened_frames - lax.optimization_barrier(jnp.mean(widened_frames, axis=-1, keepdims=True))
    inv_std = lax.rsqrt(lax.optimization_barrier(jnp.mean(center * center, axis=-1, keepdims=True)) + EPSILON)
    return (center * inv_std, inv_std)

def block_pass(frames, cotangent, valid_frame_mask, segment, weights, kernel, gain):
    row_count, length, model_width = frames.shape
    tap_count = kernel.shape[0]
    reach = tap_count // 2
    widened_frames = frames.astype(jnp.float32)
    normed, inv_std = normalize(widened_frames)
    scaled = (normed * gain).astype(jnp.bfloat16)
    flat_in = scaled.reshape(row_count * length, model_width)
    hidden = jnp.dot(flat_in, weights, preferred_element_type=jnp.float32)
    hidden = hidden.reshape(row_count, length, 2 * model_width)
    value_portion = hidden[..., :model_width]
    gate_sigmoid = jax.nn.sigmoid(hidden[..., model_width:])
    frame_validity = valid_frame_mask.astype(jnp.float32)[..., None]
    gated_linear_output = value_portion * gate_sigmoid * frame_validity
    padded = jnp.pad(gated_linear_output, ((0, 0), (reach, reach), (0, 0)))
    seg_pad = jnp.pad(segment, ((0, 0), (reach, reach)), constant_values=-1)
    convolved_frames = jnp.zeros_like(gated_linear_output)
    for offset in range(tap_count):
        window = padded[:, offset:offset + length]
        same_seg = (seg_pad[:, offset:offset + length] == segment).astype(jnp.float32)[..., None]
        convolved_frames = convolved_frames + kernel[offset] * (window * same_seg)
    swish_activation = jax.nn.sigmoid(convolved_frames)
    module_output = ((widened_frames + convolved_frames * swish_activation) * frame_validity).astype(jnp.bfloat16)
    incoming_gradient = cotangent.astype(jnp.float32) * frame_validity
    grad_conv = incoming_gradient * (swish_activation * (1.0 + convolved_frames * (1.0 - swish_activation)))
    grad_pad = jnp.pad(grad_conv, ((0, 0), (reach, reach), (0, 0)))
    gated_linear_gradient = jnp.zeros_like(gated_linear_output)
    kernel_terms = []
    for offset in range(tap_count):
        window = padded[:, offset:offset + length]
        same_seg = (seg_pad[:, offset:offset + length] == segment).astype(jnp.float32)[..., None]
        kernel_terms.append(lax.optimization_barrier(jnp.sum(grad_conv * window * same_seg, axis=(0, 1))))
        back_start = 2 * reach - offset
        back_same = (seg_pad[:, back_start:back_start + length] == segment).astype(jnp.float32)[..., None]
        gated_linear_gradient = gated_linear_gradient + kernel[offset] * (grad_pad[:, back_start:back_start + length] * back_same)
    gated_linear_gradient = gated_linear_gradient * frame_validity
    grad_hidden = jnp.concatenate([gated_linear_gradient * gate_sigmoid, gated_linear_gradient * value_portion * gate_sigmoid * (1.0 - gate_sigmoid)], axis=-1).astype(jnp.bfloat16)
    flat_grad = grad_hidden.reshape(row_count * length, 2 * model_width)
    grad_scaled = lax.dot_general(flat_grad, weights, (((1,), (1,)), ((), ())), preferred_element_type=jnp.float32)
    grad_scaled = grad_scaled.reshape(row_count, length, model_width)
    gain_term = lax.optimization_barrier(jnp.sum(grad_scaled * normed, axis=(0, 1)))
    grad_normed = grad_scaled * gain
    frame_gradient = incoming_gradient + inv_std * (grad_normed - lax.optimization_barrier(jnp.mean(grad_normed, axis=-1, keepdims=True)) - normed * lax.optimization_barrier(jnp.mean(grad_normed * normed, axis=-1, keepdims=True)))
    frame_gradient = (frame_gradient * frame_validity).astype(jnp.bfloat16)
    return (module_output, frame_gradient, flat_in, flat_grad, jnp.stack(kernel_terms), gain_term)

def reference(frames, cotangent, w_in, kernel, gain, lengths):
    positions = jnp.arange(MAXLEN, dtype=jnp.int32)
    blocks = UTTS // UTT_DEV

    def accumulate(totals, inputs):
        frame_block, cot_block, len_block = inputs
        valid_frame_mask = positions[None, :] < len_block[:, None]
        segment = jnp.where(valid_frame_mask, 0, 1).astype(jnp.int32)
        module_output, frame_gradient, flat_in, flat_grad, kernel_part, gain_part = block_pass(frame_block, cot_block, valid_frame_mask, segment, w_in, kernel, gain)
        weight_part = lax.dot_general(flat_in, flat_grad, (((0,), (0,)), ((), ())), preferred_element_type=jnp.float32)
        return ((totals[0] + weight_part, totals[1] + kernel_part, totals[2] + gain_part), (module_output, frame_gradient))
    initial = (jnp.zeros((D, 2 * D), jnp.float32), jnp.zeros((K, D), jnp.float32), jnp.zeros((D,), jnp.float32))
    totals_out, (outputs, gradients) = lax.scan(accumulate, initial, (frames.reshape(blocks, UTT_DEV, MAXLEN, D), cotangent.reshape(blocks, UTT_DEV, MAXLEN, D), lengths.reshape(blocks, UTT_DEV)))
    grad_scale = lax.rsqrt(jnp.sum(lengths).astype(jnp.float32))
    return (outputs.reshape(UTTS, MAXLEN, D), gradients.reshape(UTTS, MAXLEN, D), totals_out[0] * grad_scale, totals_out[1] * grad_scale, totals_out[2] * grad_scale)
```

```python
import functools

import jax
import jax.numpy as jnp
import numpy as np
from jax import lax
from jax.experimental import pallas as pl
from jax.experimental.pallas import tpu as pltpu
from jax.sharding import PartitionSpec as P

EPSILON = 1e-05
GROUP = 4
VMEM_LIMIT = 44 * 1024 * 1024
CHUNKS = ((0, 512), (512, 512), (1024, 512))


def split_bf16(x):
    high = x.astype(jnp.bfloat16)
    low = (x - high.astype(jnp.float32)).astype(jnp.bfloat16)
    return high, low


def time_transforms(length, taps):
    reach = taps // 2
    size = 16
    while size < length + reach:
        size *= 2
    half = size // 2
    f = np.arange(half)[:, None]
    t = np.arange(length)[None, :]
    angle = 2 * np.pi * f * t / size
    sign = np.where(np.arange(length) % 2 == 0, 1.0, -1.0)
    fwd_re, fwd_im = np.cos(angle), -np.sin(angle)
    fwd_im[0] = sign
    weight = np.where(np.arange(half) == 0, 1.0, 2.0)[:, None] / size
    inv_re, inv_im = (weight * np.cos(angle)).T, (-weight * np.sin(angle)).T
    inv_im[:, 0] = sign / size
    eye = np.eye(GROUP)
    forward = np.concatenate([np.kron(eye, fwd_re), np.kron(eye, fwd_im)], axis=0)
    inverse = np.concatenate([np.kron(eye, inv_re), np.kron(eye, inv_im)], axis=1)
    m = np.arange(taps) - reach
    tap_angle = 2 * np.pi * f * m[None, :] / size
    tap_sign = np.where(m % 2 == 0, 1.0, -1.0)
    hat_re, hat_im = np.cos(tap_angle), np.sin(tap_angle)
    hat_nyq = hat_re.copy()
    hat_nyq[0] = tap_sign
    hats = np.concatenate([hat_re, hat_im, hat_nyq], axis=0)
    back_1 = (weight * np.cos(tap_angle)).T
    back_2 = back_1.copy()
    back_2[:, 0] = tap_sign / size
    back_3 = (-weight * np.sin(tap_angle)).T
    back = np.concatenate([back_1, back_2, back_3], axis=1)
    return half, forward, inverse, hats.astype(np.float32), back.astype(np.float32)


def three_pass(matrix):
    high = matrix.astype(np.float32).astype(jnp.bfloat16)
    low = (matrix - high.astype(np.float64)).astype(np.float32).astype(jnp.bfloat16)
    return np.concatenate([high, low, high], axis=1)


def apply_three(matrix, x):
    high, low = split_bf16(x)
    return jnp.dot(
        matrix, jnp.concatenate([high, high, low], axis=0), preferred_element_type=jnp.float32
    )


def sigmoid(x):
    return 1.0 / (1.0 + jnp.exp(-x))


def chunk_kernel(red_size, half, length, has_out, idx, scaled, scaled_t, own_v, own_g, *rest):
    rest = list(rest)
    z_mine, xv, yg, z_sib, xv_sib, yg_sib = rest[:6]
    frames, cot, live, hats, fwd, inv = rest[6:12]
    rest = rest[12 + has_out :]
    out, keep, send, gh, w, sums = rest
    core, quarter, red, parity = idx[0], idx[1], idx[2], idx[3]
    width = own_v.shape[1]
    block = own_v.shape[0]
    part = block // 4

    def place(s, par, cor, v, g):
        owner = lax.rem(red + red_size - s, red_size)
        row = pl.multiple_of(owner * block + (par * 2 + cor) * part, 16)
        w[pl.ds(row, part), :width] = v
        w[pl.ds(row, part), width:] = g

    own_row = pl.multiple_of(red * block, 16)
    w[pl.ds(own_row, block), :width] = own_v[...]
    w[pl.ds(own_row, block), width:] = own_g[...]
    for s in range(1, red_size):
        place(s, parity, core, z_mine[s - 1, :, :width], z_mine[s - 1, :, width:])
        place(s, 1 - parity, core, xv[s - 1], yg[s - 1])
        place(s, parity, 1 - core, z_sib[s - 1, :, :width], z_sib[s - 1, :, width:])
        place(s, 1 - parity, 1 - core, xv_sib[s - 1], yg_sib[s - 1])

    rows = GROUP * length
    hat_a, hat_b, hat_c = hats[0], hats[1], hats[2]
    total = [jnp.zeros((half, width), jnp.float32) for _ in range(3)]
    for group in range(scaled.shape[0] // rows):
        at = pl.ds(group * rows, rows)
        hidden = jnp.dot(scaled[at, :], w[...], preferred_element_type=jnp.float32)
        alive = jnp.concatenate([live[at, :]] * (width // 128), axis=1)
        value = hidden[:, :width]
        gate = sigmoid(hidden[:, width:])
        glu = value * gate * alive
        x_hat = apply_three(fwd[...], glu).reshape(2, GROUP, half, width)
        x_re, x_im = x_hat[0], x_hat[1]
        y_hat = jnp.concatenate(
            [
                (x_re * hat_a - x_im * hat_b).reshape(GROUP * half, width),
                (x_re * hat_b + x_im * hat_c).reshape(GROUP * half, width),
            ],
            axis=0,
        )
        conv = apply_three(inv[...], y_hat)
        s = sigmoid(conv)
        out[at, :] = ((frames[at, :].astype(jnp.float32) + conv * s) * alive).astype(out.dtype)
        grad_conv = cot[at, :].astype(jnp.float32) * alive * (s * (1.0 + conv * (1.0 - s)))
        g_hat = apply_three(fwd[...], grad_conv).reshape(2, GROUP, half, width)
        g_re, g_im = g_hat[0], g_hat[1]
        total[0] = total[0] + jnp.sum(g_re * x_re, axis=0)
        total[1] = total[1] + jnp.sum(g_im * x_im, axis=0)
        total[2] = total[2] + jnp.sum(g_re * x_im - g_im * x_re, axis=0)
        back_hat = jnp.concatenate(
            [
                (g_re * hat_a + g_im * hat_b).reshape(GROUP * half, width),
                (g_im * hat_c - g_re * hat_b).reshape(GROUP * half, width),
            ],
            axis=0,
        )
        grad_glu = apply_three(inv[...], back_hat) * alive
        grad_v = grad_glu * gate
        gh[0, at, :] = grad_v.astype(jnp.bfloat16)
        gh[1, at, :] = (grad_v * value * (1.0 - gate)).astype(jnp.bfloat16)
    sums[...] = jnp.concatenate(total, axis=0)

    for dest, which in ((send, 1 - core), (keep, core)):
        grad = gh[which]
        for b in range(red_size):
            slot = lax.rem(b + red_size - red, red_size)
            res = jnp.dot(
                scaled_t[b * block : (b + 1) * block, :], grad, preferred_element_type=jnp.float32
            ).astype(jnp.bfloat16)
            for q in range(4):
                dest[lax.bitwise_xor(q, quarter), slot] = res[q * part : (q + 1) * part]


def frame_kernel(n_chunks, scaled_inv, frames, cot, live, gain, *rest):
    ghs, ws = rest[:n_chunks], rest[n_chunks : 2 * n_chunks]
    out, gain_sum = rest[2 * n_chunks :]
    model_width = frames.shape[1]
    grad_scaled = None
    for gh, w in zip(ghs, ws):
        width = w.shape[1] // 2
        for part in range(2):
            term = lax.dot_general(
                gh[part],
                w[:, part * width : (part + 1) * width],
                (((1,), (1,)), ((), ())),
                preferred_element_type=jnp.float32,
            )
            grad_scaled = term if grad_scaled is None else grad_scaled + term
    wide = frames[...].astype(jnp.float32)
    center = wide - jnp.mean(wide, axis=-1, keepdims=True)
    inv_std = lax.rsqrt(jnp.mean(center * center, axis=-1, keepdims=True) + EPSILON)
    normed = center * inv_std
    prod = grad_scaled * normed
    part_sum = jnp.sum(prod.reshape(-1, 8, model_width), axis=0)

    @pl.when(pl.program_id(0) == 0)
    def _():
        gain_sum[...] = part_sum

    @pl.when(pl.program_id(0) != 0)
    def _():
        gain_sum[...] += part_sum

    grad_normed = grad_scaled * gain[...]
    alive = jnp.concatenate([live[...]] * (model_width // 128), axis=1)
    upstream = cot[...].astype(jnp.float32) * alive
    res = upstream + inv_std * (
        grad_normed
        - jnp.mean(grad_normed, axis=-1, keepdims=True)
        - normed * jnp.mean(grad_normed * normed, axis=-1, keepdims=True)
    )
    out[...] = (res * alive).astype(out.dtype)


def place_kernel(has_out, idx, mine, sib, *rest):
    out = rest[has_out]
    core, quarter = idx[0], idx[1]
    part = mine.shape[1]

    def write(src):
        for r in range(4):
            q = lax.bitwise_xor(r, quarter)
            out[pl.ds(pl.multiple_of(q * part, 16), part), :] = src[r].astype(jnp.float32)

    own = pl.program_id(0) == core
    pl.when(own)(lambda: write(mine))
    pl.when(jnp.logical_not(own))(lambda: write(sib))


def vmem(n):
    return [pl.BlockSpec(memory_space=pltpu.VMEM) for _ in range(n)]


def tree_sum(terms):
    if len(terms) == 1:
        return terms[0]
    return tree_sum(terms[::2]) + tree_sum(terms[1::2])


def local(frames, cotangent, w_in, kernel, gain, lengths):
    dp_size = lax.axis_size("dp")
    red_size = lax.axis_size("red")
    dp = lax.axis_index("dp")
    red = lax.axis_index("red")
    local_utts, length, model_width = frames.shape
    taps = kernel.shape[0]
    block = model_width // red_size
    part = block // 4
    n_rows = local_utts * length

    core = dp % 2
    quarter = (dp // 2) % 4
    parity = (quarter + quarter // 2) % 2
    idx = jnp.stack([core, quarter, red, parity]).astype(jnp.int32)

    def to_core(x):
        return lax.ppermute(x, "dp", [(i, i ^ 1) for i in range(dp_size)])

    def to_quarter(x, r):
        return lax.ppermute(x, "dp", [(i, i ^ (2 * r)) for i in range(dp_size)])

    def shift_red(x, s):
        return lax.ppermute(x, "red", [(i, (i + s) % red_size) for i in range(red_size)])

    def other_groups(x):
        bit = 8
        while bit < dp_size:
            x = x + lax.ppermute(x, "dp", [(i, i ^ bit) for i in range(dp_size)])
            bit *= 2
        return x

    half, forward, inverse, hat_matrix, back_matrix = time_transforms(length, taps)
    fwd3, inv3 = jnp.asarray(three_pass(forward)), jnp.asarray(three_pass(inverse))

    piece = lax.dynamic_slice(w_in, ((parity * 2 + core) * part, 0), (part, 2 * model_width))
    gathered = []
    for start, width in CHUNKS:
        gate_start = model_width + start
        mine = jnp.concatenate(
            [piece[:, start : start + width], piece[:, gate_start : gate_start + width]], axis=1
        )
        z_mine = jnp.stack([shift_red(mine, s) for s in range(1, red_size)])
        z_sib = to_core(z_mine)
        xv = to_quarter(z_mine[:, :, :width], 1)
        yg = to_quarter(z_mine[:, :, width:], 2)
        xv_sib, yg_sib = to_core(xv), to_core(yg)
        own_v = w_in[:, start : start + width]
        own_g = w_in[:, gate_start : gate_start + width]
        gathered.append((own_v, own_g, z_mine, xv, yg, z_sib, xv_sib, yg_sib))

    flat_frames = frames.reshape(n_rows, model_width)
    flat_cot = cotangent.reshape(n_rows, model_width)
    wide = flat_frames.astype(jnp.float32)
    center = wide - jnp.mean(wide, axis=-1, keepdims=True)
    inv_std = lax.rsqrt(jnp.mean(center * center, axis=-1, keepdims=True) + EPSILON)
    scaled = (center * inv_std * gain).astype(jnp.bfloat16)
    scaled_t = scaled.T
    own_lengths = lax.dynamic_slice(
        lengths.reshape(dp_size, red_size, local_utts), (dp, red, 0), (1, 1, local_utts)
    ).reshape(local_utts)
    alive = (jnp.arange(length, dtype=jnp.int32)[None, :] < own_lengths[:, None]).astype(jnp.float32)
    live = jnp.broadcast_to(alive.reshape(n_rows, 1), (n_rows, 128))
    root = lax.rsqrt(jnp.sum(lengths).astype(jnp.float32))
    hats = jnp.dot(hat_matrix, kernel, precision=lax.Precision.HIGHEST).reshape(3, half, model_width)

    out = None
    grad_out = None
    ghs, ws, sums = [], [], []
    for (start, width), weights in zip(CHUNKS, gathered):
        column = start // width
        strip = pl.BlockSpec((n_rows, width), lambda i, column=column: (0, column))
        has_out = 0 if out is None else 1
        operands = [idx, scaled, scaled_t, *weights, flat_frames, flat_cot, live, hats, fwd3, inv3]
        in_specs = [pl.BlockSpec(memory_space=pltpu.SMEM), *vmem(10), strip, strip, *vmem(1)]
        in_specs += [
            pl.BlockSpec((3, half, width), lambda i, column=column: (0, 0, column)),
            *vmem(2),
        ]
        aliases = {}
        if has_out:
            aliases = {len(operands): 0}
            operands.append(out)
            in_specs.append(pl.BlockSpec(memory_space=pl.ANY))
        flops = 2 * n_rows * model_width * width * 4 + 2 * 12 * 256 * n_rows * width
        out, keep, send, gh, w, tap_sums = pl.pallas_call(
            functools.partial(chunk_kernel, red_size, half, length, has_out),
            grid=(1,),
            in_specs=in_specs,
            out_specs=[strip, *vmem(5)],
            out_shape=[
                jax.ShapeDtypeStruct((n_rows, model_width), jnp.bfloat16),
                jax.ShapeDtypeStruct((4, red_size, part, width), jnp.bfloat16),
                jax.ShapeDtypeStruct((4, red_size, part, width), jnp.bfloat16),
                jax.ShapeDtypeStruct((2, n_rows, width), jnp.bfloat16),
                jax.ShapeDtypeStruct((model_width, 2 * width), jnp.bfloat16),
                jax.ShapeDtypeStruct((3 * half, width), jnp.float32),
            ],
            input_output_aliases=aliases,
            compiler_params=pltpu.CompilerParams(vmem_limit_bytes=VMEM_LIMIT),
            cost_estimate=pl.CostEstimate(
                flops=flops, bytes_accessed=24 * 1024 * width, transcendentals=4 * n_rows * width
            ),
        )(*operands)
        ghs.append(gh)
        ws.append(w)
        sums.append(tap_sums)

        pair = keep.astype(jnp.float32) + to_core(send).astype(jnp.float32)
        pair = pair.astype(jnp.bfloat16)
        parts = [pair[0], *(to_quarter(pair[r], r) for r in range(1, 4))]
        plane = tree_sum([p.astype(jnp.float32) for p in parts]).astype(jnp.bfloat16)
        parts = [plane[0], *(shift_red(plane[s], s) for s in range(1, red_size))]
        owned = other_groups(tree_sum([p.astype(jnp.float32) for p in parts]))
        owned = (owned * root).astype(jnp.bfloat16)
        mine = jnp.stack([owned, *(to_quarter(owned, r) for r in range(1, 4))])
        sib = to_core(mine)
        has_out = 0 if grad_out is None else 1
        operands = [idx, mine, sib] + ([grad_out] if has_out else [])
        half_step = model_width // width
        grad_out = pl.pallas_call(
            functools.partial(place_kernel, has_out),
            grid=(2,),
            in_specs=[
                pl.BlockSpec(memory_space=pltpu.SMEM),
                *vmem(2),
                *([pl.BlockSpec(memory_space=pl.ANY)] if has_out else []),
            ],
            out_specs=pl.BlockSpec(
                (block, width),
                lambda i, column=column, half_step=half_step: (0, column + i * half_step),
            ),
            out_shape=jax.ShapeDtypeStruct((block, 2 * model_width), jnp.float32),
            input_output_aliases={3: 0} if has_out else {},
            cost_estimate=pl.CostEstimate(
                flops=0, bytes_accessed=12 * block * width, transcendentals=0
            ),
        )(*operands)

    step = GROUP * length
    row_spec = pl.BlockSpec((step, model_width), lambda i: (i, 0))
    frame_gradient, gain_part = pl.pallas_call(
        functools.partial(frame_kernel, len(CHUNKS), None),
        grid=(n_rows // step,),
        in_specs=[
            row_spec,
            row_spec,
            pl.BlockSpec((step, 128), lambda i: (i, 0)),
            *vmem(1),
            *(pl.BlockSpec((2, step, width), lambda i: (0, i, 0)) for _, width in CHUNKS),
            *vmem(len(CHUNKS)),
        ],
        out_specs=[row_spec, pl.BlockSpec((8, model_width), lambda i: (0, 0))],
        out_shape=[
            jax.ShapeDtypeStruct((n_rows, model_width), jnp.bfloat16),
            jax.ShapeDtypeStruct((8, model_width), jnp.float32),
        ],
        compiler_params=pltpu.CompilerParams(vmem_limit_bytes=VMEM_LIMIT),
        cost_estimate=pl.CostEstimate(
            flops=4 * n_rows * model_width * model_width,
            bytes_accessed=24 * 1024 * 1024,
            transcendentals=0,
        ),
    )(flat_frames, flat_cot, live, gain.reshape(1, model_width), *ghs, *ws)

    order = sorted(range(len(CHUNKS)), key=lambda c: CHUNKS[c][0])
    tap_part = jnp.dot(
        back_matrix,
        jnp.concatenate([sums[c] for c in order], axis=1),
        precision=lax.Precision.HIGHEST,
    )
    small = jnp.concatenate([tap_part, jnp.sum(gain_part, axis=0, keepdims=True)], axis=0)
    side = model_width // 2
    small = small.reshape(taps + 1, 2, side)
    kept = lax.dynamic_index_in_dim(small, core, 1, keepdims=False)
    sent = lax.dynamic_index_in_dim(small, 1 - core, 1, keepdims=False)
    kept = kept + to_core(sent)
    kept = tree_sum([kept, *(to_quarter(kept, r) for r in range(1, 4))])
    kept = tree_sum([kept, *(shift_red(kept, s) for s in range(1, red_size))])
    kept = other_groups(kept) * root
    other = to_core(kept)
    first = core == 0
    small = jnp.concatenate([jnp.where(first, kept, other), jnp.where(first, other, kept)], axis=1)
    return (
        out.reshape(frames.shape),
        frame_gradient.reshape(frames.shape),
        grad_out,
        small[:taps],
        small[taps],
    )


def solution(mesh):
    placed = (
        P(("dp", "red"), None, None),
        P(("dp", "red"), None, None),
        P("red", None),
        P(),
        P(),
        P(),
    )
    return jax.shard_map(
        local,
        mesh=mesh,
        in_specs=placed,
        out_specs=(
            P(("dp", "red"), None, None),
            P(("dp", "red"), None, None),
            P("red", None),
            P(),
            P(),
        ),
        check_vma=False,
    )
```

```python
import functools

import jax
import jax.numpy as jnp
import numpy as np
from jax import lax
from jax.experimental import pallas as pl
from jax.experimental.pallas import tpu as pltpu
from jax.sharding import PartitionSpec as P

EPSILON = 1e-05
GROUP = 4
VMEM_LIMIT = 48 * 1024 * 1024
CHUNKS = ((0, 256), (256, 256), (512, 256))


def split_bf16(x):
    high = x.astype(jnp.bfloat16)
    low = (x - high.astype(jnp.float32)).astype(jnp.bfloat16)
    return high, low


def time_transforms(length, taps):
    reach = taps // 2
    size = 16
    while size < length + reach:
        size *= 2
    half = size // 2
    f = np.arange(half)[:, None]
    t = np.arange(length)[None, :]
    angle = 2 * np.pi * f * t / size
    sign = np.where(np.arange(length) % 2 == 0, 1.0, -1.0)
    fwd_re, fwd_im = np.cos(angle), -np.sin(angle)
    fwd_im[0] = sign
    weight = np.where(np.arange(half) == 0, 1.0, 2.0)[:, None] / size
    inv_re, inv_im = (weight * np.cos(angle)).T, (-weight * np.sin(angle)).T
    inv_im[:, 0] = sign / size
    eye = np.eye(GROUP)
    forward = np.concatenate([np.kron(eye, fwd_re), np.kron(eye, fwd_im)], axis=0)
    inverse = np.concatenate([np.kron(eye, inv_re), np.kron(eye, inv_im)], axis=1)
    m = np.arange(taps) - reach
    tap_angle = 2 * np.pi * f * m[None, :] / size
    tap_sign = np.where(m % 2 == 0, 1.0, -1.0)
    hat_re, hat_im = np.cos(tap_angle), np.sin(tap_angle)
    hat_nyq = hat_re.copy()
    hat_nyq[0] = tap_sign
    hats = np.concatenate([hat_re, hat_im, hat_nyq], axis=0)
    back_1 = (weight * np.cos(tap_angle)).T
    back_2 = back_1.copy()
    back_2[:, 0] = tap_sign / size
    back_3 = (-weight * np.sin(tap_angle)).T
    back = np.concatenate([back_1, back_2, back_3], axis=1)
    return half, forward, inverse, hats.astype(np.float32), back.astype(np.float32)


def three_pass(matrix):
    high = matrix.astype(np.float32).astype(jnp.bfloat16)
    low = (matrix - high.astype(np.float64)).astype(np.float32).astype(jnp.bfloat16)
    return np.concatenate([high, low, high], axis=1)


def three_terms(x):
    high, low = split_bf16(x)
    return jnp.concatenate([high, high, low], axis=0)


def sigmoid(x):
    return 1.0 / (1.0 + jnp.exp(-x))


def scale_kernel(own, sib, gain, scaled, scaled_t):
    def run(frames):
        wide = frames[...].astype(jnp.float32)
        center = wide - jnp.mean(wide, axis=-1, keepdims=True)
        inv_std = lax.rsqrt(jnp.mean(center * center, axis=-1, keepdims=True) + EPSILON)
        res = (center * inv_std * gain[...]).astype(jnp.bfloat16)
        scaled[...] = res
        scaled_t[...] = res.T

    first = pl.program_id(0) < pl.num_programs(0) // 2
    pl.when(first)(lambda: run(own))
    pl.when(jnp.logical_not(first))(lambda: run(sib))


def chunk_kernel(red_size, length, start, has_out, idx, *rest):
    rest = list(rest)
    scaled_hbm, scaled_t_hbm, w_in = rest[:3]
    z_parts, rest = rest[3 : 2 + red_size], rest[2 + red_size :]
    xv, yg, frames_own, frames_sib, cot_own, cot_sib, live, hats, fwd, inv = rest[:10]
    rest = rest[10 + 2 * has_out :]
    out_own, out_sib, grads, gh, w_out, sums = rest[0], rest[1], rest[2:6], *rest[6:9]
    scaled, scaled_t, w, grad, sem_w, sem_s, sem_t, sem_o, sem_g = rest[9:]
    core, quarter, red, parity = idx[0], idx[1], idx[2], idx[3]
    n_rows, model_width = scaled.shape
    width = w.shape[1] // 2
    block = model_width // red_size
    half_block, part = block // 2, block // 4
    half = hats.shape[1]

    copies = []

    def fetch(src, row, rows, column):
        row = pl.multiple_of(row, 16)
        dst = w.at[pl.ds(row, rows), column : column + src.shape[-1]]
        copies.append(pltpu.make_async_copy(src, dst, sem_w.at[len(copies)]))

    for side in range(2):
        column = pl.multiple_of(core * (model_width // 2) + side * model_width + start, 128)
        fetch(w_in.at[:, pl.ds(column, width)], red * block, block, side * width)
    for s in range(1, red_size):
        row = lax.rem(red + red_size - s, red_size) * block
        fetch(z_parts[s - 1], row + parity * half_block, half_block, 0)
        fetch(xv.at[s - 1], row + (1 - parity) * half_block, half_block, 0)
        fetch(yg.at[s - 1], row + (1 - parity) * half_block, half_block, width)
    get_scaled = pltpu.make_async_copy(scaled_hbm, scaled, sem_s)
    get_scaled_t = pltpu.make_async_copy(scaled_t_hbm, scaled_t, sem_t)
    for copy in copies:
        copy.start()
    get_scaled.start()
    get_scaled_t.start()
    for copy in copies:
        copy.wait()
    put_w = pltpu.make_async_copy(w, w_out, sem_o)
    put_w.start()
    get_scaled.wait()

    rows = GROUP * length
    per_core = n_rows // rows // 2
    hat_a, hat_b, hat_c = hats[0], hats[1], hats[2]
    sums[...] = jnp.zeros_like(sums)

    def stages(group):
        at = pl.ds(group * rows, rows)
        local_at = pl.ds(group % per_core * rows, rows)
        if group < per_core:
            frames, cot, out = frames_own, cot_own, out_own
        else:
            frames, cot, out = frames_sib, cot_sib, out_sib

        def alive():
            return jnp.concatenate([live[at, :]] * (width // 128), axis=1)

        hidden = jnp.dot(scaled[at, :], w[...], preferred_element_type=jnp.float32)
        yield
        value = hidden[:, :width]
        gate = sigmoid(hidden[:, width:])
        terms = three_terms(value * gate * alive())
        yield
        x_hat = jnp.dot(fwd[...], terms, preferred_element_type=jnp.float32)
        yield
        x_hat = x_hat.reshape(2, GROUP, half, width)
        x_re, x_im = x_hat[0], x_hat[1]
        terms = three_terms(
            jnp.concatenate(
                [
                    (x_re * hat_a - x_im * hat_b).reshape(GROUP * half, width),
                    (x_re * hat_b + x_im * hat_c).reshape(GROUP * half, width),
                ],
                axis=0,
            )
        )
        yield
        conv = jnp.dot(inv[...], terms, preferred_element_type=jnp.float32)
        yield
        s = sigmoid(conv)
        wide = frames[local_at, :].astype(jnp.float32)
        out[local_at, :] = ((wide + conv * s) * alive()).astype(out.dtype)
        upstream = cot[local_at, :].astype(jnp.float32) * alive()
        terms = three_terms(upstream * (s * (1.0 + conv * (1.0 - s))))
        yield
        g_hat = jnp.dot(fwd[...], terms, preferred_element_type=jnp.float32)
        yield
        g_hat = g_hat.reshape(2, GROUP, half, width)
        g_re, g_im = g_hat[0], g_hat[1]
        sums[:half] += jnp.sum(g_re * x_re, axis=0)
        sums[half : 2 * half] += jnp.sum(g_im * x_im, axis=0)
        sums[2 * half :] += jnp.sum(g_re * x_im - g_im * x_re, axis=0)
        terms = three_terms(
            jnp.concatenate(
                [
                    (g_re * hat_a + g_im * hat_b).reshape(GROUP * half, width),
                    (g_im * hat_c - g_re * hat_b).reshape(GROUP * half, width),
                ],
                axis=0,
            )
        )
        yield
        grad_glu = jnp.dot(inv[...], terms, preferred_element_type=jnp.float32)
        yield
        grad_v = grad_glu * alive() * gate
        gh[at, :width] = grad_v.astype(jnp.bfloat16)
        gh[at, width:] = (grad_v * value * (1.0 - gate)).astype(jnp.bfloat16)

    running = [stages(group) for group in range(2 * per_core)]
    turn = 0
    while any(g is not None for g in running):
        for group in range(min(turn + 1, len(running))):
            if running[group] is not None:
                try:
                    next(running[group])
                except StopIteration:
                    running[group] = None
        turn += 1

    get_scaled_t.wait()
    sends = []
    for b in range(red_size):
        grad[pl.ds(b * block, block), :] = jnp.dot(
            scaled_t[pl.ds(b * block, block), :], gh[...], preferred_element_type=jnp.float32
        ).astype(jnp.bfloat16)
        slot = lax.rem(b + red_size - red, red_size)
        for r in range(4):
            row = pl.multiple_of(b * block + lax.bitwise_xor(quarter, r) * part, 16)
            copy = pltpu.make_async_copy(
                grad.at[pl.ds(row, part), :], grads[r].at[slot], sem_g.at[len(sends)]
            )
            copy.start()
            sends.append(copy)
    for copy in sends:
        copy.wait()
    put_w.wait()


def plane_kernel(*refs):
    parts, outs = refs[:4], refs[4:]
    for s, out in enumerate(outs):
        terms = [p[s].astype(jnp.float32) for p in parts]
        out[...] = tree_sum(terms).astype(out.dtype)


def grad_scaled_kernel(n_chunks, *refs):
    ghs, ws, out = refs[:n_chunks], refs[n_chunks : 2 * n_chunks], refs[2 * n_chunks]
    out[...] = scaled_gradient(ghs, ws).astype(out.dtype)


def scaled_gradient(ghs, ws):
    total = None
    for gh, w in zip(ghs, ws):
        term = lax.dot_general(
            gh[...], w[...], (((1,), (1,)), ((), ())), preferred_element_type=jnp.float32
        )
        total = term if total is None else total + term
    return total


def frame_kernel(n_chunks, idx, frames, cot, live, gain, other, out_mine, out_other, *rest):
    ghs, ws = rest[:n_chunks], rest[n_chunks : 2 * n_chunks]
    out, frame_out, gain_sum = rest[2 * n_chunks :]
    model_width = frames.shape[1]
    side = model_width // 2
    mine = pl.multiple_of(idx[0] * side, 128)
    out[:, pl.ds(mine, side)] = out_mine[...]
    out[:, pl.ds(pl.multiple_of(side - mine, 128), side)] = out_other[...]
    grad_scaled = scaled_gradient(ghs, ws) + other[...].astype(jnp.float32)
    wide = frames[...].astype(jnp.float32)
    center = wide - jnp.mean(wide, axis=-1, keepdims=True)
    inv_std = lax.rsqrt(jnp.mean(center * center, axis=-1, keepdims=True) + EPSILON)
    normed = center * inv_std
    part_sum = jnp.sum((grad_scaled * normed).reshape(-1, 8, model_width), axis=0)

    @pl.when(pl.program_id(0) == 0)
    def _():
        gain_sum[...] = part_sum

    @pl.when(pl.program_id(0) != 0)
    def _():
        gain_sum[...] += part_sum

    grad_normed = grad_scaled * gain[...]
    alive = jnp.concatenate([live[...]] * (model_width // 128), axis=1)
    upstream = cot[...].astype(jnp.float32) * alive
    res = upstream + inv_std * (
        grad_normed
        - jnp.mean(grad_normed, axis=-1, keepdims=True)
        - normed * jnp.mean(grad_normed * normed, axis=-1, keepdims=True)
    )
    frame_out[...] = (res * alive).astype(frame_out.dtype)


def place_kernel(has_out, idx, mine, sib, *rest):
    out = rest[has_out]
    quarter = idx[1]
    part = mine.shape[1]
    side = pl.program_id(1)
    width = out.shape[1]

    def write(src):
        for r in range(4):
            q = lax.bitwise_xor(r, quarter)
            row = pl.ds(pl.multiple_of(q * part, 16), part)
            out[row, :] = src[r, :, pl.ds(pl.multiple_of(side * width, 128), width)].astype(jnp.float32)

    own = pl.program_id(0) == idx[0]
    pl.when(own)(lambda: write(mine))
    pl.when(jnp.logical_not(own))(lambda: write(sib))


def pack_first_kernel(idx, values, gates, out):
    width = values.shape[1]
    out[:, :width] = values[...]
    out[:, width:] = gates[...]


def pack_second_kernel(n, *refs):
    parts, (out_v, out_g) = refs[:n], refs[n:]
    width = out_v.shape[2]
    for s in range(n):
        out_v[s] = parts[s][:, :width]
        out_g[s] = parts[s][:, width:]


def line_kernel(n, root, *refs):
    terms = [part[...].astype(jnp.float32) for part in refs[:n]]
    refs[n][...] = (tree_sum(terms) * root[0]).astype(refs[n].dtype)


def ordered(body, n_in, n_after):
    def kernel(*refs):
        return body(*refs[:n_in], *refs[n_in + n_after :])

    return kernel


def tree_sum(terms):
    if len(terms) == 1:
        return terms[0]
    return tree_sum(terms[::2]) + tree_sum(terms[1::2])


def whole(shape):
    return pl.BlockSpec(shape, lambda *_: (0,) * len(shape))


def params():
    return pltpu.CompilerParams(vmem_limit_bytes=VMEM_LIMIT)


def cost(flops, moved, transcendentals=0):
    return pl.CostEstimate(flops=flops, bytes_accessed=moved, transcendentals=transcendentals)


ANY = pl.BlockSpec(memory_space=pltpu.HBM)


def local(frames, cotangent, w_in, kernel, gain, lengths):
    dp_size = lax.axis_size("dp")
    red_size = lax.axis_size("red")
    dp = lax.axis_index("dp")
    red = lax.axis_index("red")
    local_utts, length, model_width = frames.shape
    taps = kernel.shape[0]
    block = model_width // red_size
    part = block // 4
    side = model_width // 2
    own_rows = local_utts * length
    n_rows = 2 * own_rows
    n_chunks = len(CHUNKS)

    core = dp % 2
    quarter = (dp // 2) % 4
    parity = (quarter + quarter // 2) % 2
    idx = jnp.stack([core, quarter, red, parity]).astype(jnp.int32)

    def to_core(x):
        return lax.ppermute(x, "dp", [(i, i ^ 1) for i in range(dp_size)])

    def to_quarter(x, r):
        return lax.ppermute(x, "dp", [(i, i ^ (2 * r)) for i in range(dp_size)])

    def shift_red(x, s):
        return lax.ppermute(x, "red", [(i, (i + s) % red_size) for i in range(red_size)])

    def other_groups(x):
        bit = 8
        while bit < dp_size:
            x = x + lax.ppermute(x, "dp", [(i, i ^ bit) for i in range(dp_size)])
            bit *= 2
        return x

    half, forward, inverse, hat_matrix, back_matrix = time_transforms(length, taps)
    fwd3, inv3 = jnp.asarray(three_pass(forward)), jnp.asarray(three_pass(inverse))

    flat_frames = frames.reshape(own_rows, model_width)
    flat_cot = cotangent.reshape(own_rows, model_width)

    def first_sends(chunk, *deps):
        start, width = CHUNKS[chunk]
        column, columns = start // width, side // width

        def strip(which):
            return pl.BlockSpec(
                (block // 2, width),
                lambda i, idx: (idx[3], idx[0] * columns + column + which * 2 * columns),
            )

        mine = pl.pallas_call(
            ordered(pack_first_kernel, 3, len(deps)),
            grid_spec=pltpu.PrefetchScalarGridSpec(
                num_scalar_prefetch=1,
                grid=(1,),
                in_specs=[strip(0), strip(1)] + [ANY] * len(deps),
                out_specs=whole((block // 2, 2 * width)),
            ),
            out_shape=jax.ShapeDtypeStruct((block // 2, 2 * width), jnp.bfloat16),
            compiler_params=params(),
            cost_estimate=cost(0, 4 * block * width),
        )(idx, w_in, w_in, *deps)
        return mine, [shift_red(mine, s) for s in range(1, red_size)]

    def second_pack(z_parts, *deps):
        n = len(z_parts)
        width = z_parts[0].shape[1] // 2
        shape = (n, block // 2, width)
        return pl.pallas_call(
            ordered(functools.partial(pack_second_kernel, n), n, len(deps)),
            grid=(1,),
            in_specs=[whole(z_parts[0].shape)] * n + [ANY] * len(deps),
            out_specs=[whole(shape)] * 2,
            out_shape=[jax.ShapeDtypeStruct(shape, jnp.bfloat16)] * 2,
            compiler_params=params(),
            cost_estimate=cost(0, 4 * n * block * width),
        )(*z_parts, *deps)

    def second_sends(packed):
        return to_quarter(packed[0], 1), to_quarter(packed[1], 2)

    mine, z_first = first_sends(0)
    z = [z_first]
    sib_frames, sib_cot = to_core(flat_frames), to_core(flat_cot)

    tile = 256
    tiles = own_rows // tile
    scaled, scaled_t = pl.pallas_call(
        ordered(scale_kernel, 3, 1),
        grid=(2 * tiles,),
        in_specs=[
            pl.BlockSpec((tile, model_width), lambda i: (jnp.minimum(i, tiles - 1), 0)),
            pl.BlockSpec((tile, model_width), lambda i: (jnp.maximum(i - tiles, 0), 0)),
            whole((1, model_width)),
            ANY,
        ],
        out_specs=[
            pl.BlockSpec((tile, model_width), lambda i: (i, 0)),
            pl.BlockSpec((model_width, tile), lambda i: (0, i)),
        ],
        out_shape=[
            pltpu.HBM((n_rows, model_width), jnp.bfloat16),
            pltpu.HBM((model_width, n_rows), jnp.bfloat16),
        ],
        compiler_params=params(),
        cost_estimate=cost(10 * n_rows * model_width, 6 * n_rows * model_width),
    )(flat_frames, sib_frames, gain.reshape(1, model_width), mine)

    packed = [second_pack(z[0], scaled)]
    near = [second_sends(packed[0])]
    firsts = []
    for chunk in range(1, n_chunks):
        mine, z_next = first_sends(chunk, *z[-1], *([scaled] if chunk == 1 else []))
        z.append(z_next)
        firsts.append(mine)
    if n_chunks > 1:
        packed.append(second_pack(z[1], *near[0]))
        near.append(second_sends(packed[1]))

    by_owner = lengths.reshape(dp_size, red_size, local_utts)

    def alive_rows(device):
        own = lax.dynamic_slice(by_owner, (device, red, 0), (1, 1, local_utts)).reshape(local_utts)
        return jnp.arange(length, dtype=jnp.int32)[None, :] < own[:, None]

    alive = jnp.stack([alive_rows(dp), alive_rows(dp + 1 - 2 * core)]).astype(jnp.float32)
    live = jnp.broadcast_to(alive.reshape(n_rows, 1), (n_rows, 128))
    root = lax.rsqrt(jnp.sum(lengths).astype(jnp.float32))
    hats = jnp.dot(hat_matrix, kernel, precision=lax.Precision.HIGHEST).reshape(3, half, model_width)

    def middle(chunk, outs, deps):
        start, width = CHUNKS[chunk]
        near_column = start // width
        columns = side // width

        def strip(*leading):
            return pl.BlockSpec(
                (*leading, width),
                lambda i, idx: (*(0 for _ in leading), idx[0] * columns + near_column),
            )

        operands = [scaled, scaled_t, w_in, *z[chunk], *near[chunk]]
        in_specs = [ANY] * len(operands)
        operands += [flat_frames, sib_frames, flat_cot, sib_cot, live, hats, fwd3, inv3]
        in_specs += [strip(own_rows)] * 4
        in_specs += [whole((n_rows, 128)), strip(3, half), whole(fwd3.shape), whole(inv3.shape)]
        aliases = {}
        if outs is not None:
            aliases = {len(operands) + 1: 0, len(operands) + 2: 1}
            operands += outs
            in_specs += [ANY] * 2
        n_in = len(operands) + 1
        operands += deps
        in_specs += [ANY] * len(deps)
        near_strip = pl.BlockSpec((own_rows, width), lambda i, idx: (0, near_column))
        return pl.pallas_call(
            ordered(
                functools.partial(chunk_kernel, red_size, length, start, 1 if aliases else 0),
                n_in,
                len(deps),
            ),
            grid_spec=pltpu.PrefetchScalarGridSpec(
                num_scalar_prefetch=1,
                grid=(1,),
                in_specs=in_specs,
                out_specs=[near_strip, near_strip]
                + [ANY] * 4
                + [whole((n_rows, 2 * width)), ANY, whole((3 * half, width))],
                scratch_shapes=[
                    pltpu.VMEM((n_rows, model_width), jnp.bfloat16),
                    pltpu.VMEM((model_width, n_rows), jnp.bfloat16),
                    pltpu.VMEM((model_width, 2 * width), jnp.bfloat16),
                    pltpu.VMEM((model_width, 2 * width), jnp.bfloat16),
                    pltpu.SemaphoreType.DMA((3 * red_size - 1,)),
                    pltpu.SemaphoreType.DMA,
                    pltpu.SemaphoreType.DMA,
                    pltpu.SemaphoreType.DMA,
                    pltpu.SemaphoreType.DMA((4 * red_size,)),
                ],
            ),
            out_shape=[
                pltpu.HBM((own_rows, side), jnp.bfloat16),
                pltpu.HBM((own_rows, side), jnp.bfloat16),
                *[jax.ShapeDtypeStruct((red_size, part, 2 * width), jnp.bfloat16)] * 4,
                pltpu.HBM((n_rows, 2 * width), jnp.bfloat16),
                jax.ShapeDtypeStruct((model_width, 2 * width), jnp.bfloat16),
                jax.ShapeDtypeStruct((3 * half, width), jnp.float32),
            ],
            input_output_aliases=aliases,
            compiler_params=params(),
            cost_estimate=cost(
                8 * n_rows * model_width * width + 24 * 256 * n_rows * width, 1 << 24, 4 * n_rows * width
            ),
        )(idx, *operands)

    def add_plane(parts, *deps):
        shape = parts[0].shape
        return pl.pallas_call(
            ordered(plane_kernel, 4, len(deps)),
            grid=(1,),
            in_specs=[whole(shape)] * 4 + [ANY] * len(deps),
            out_specs=[whole(shape[1:])] * red_size,
            out_shape=[jax.ShapeDtypeStruct(shape[1:], jnp.bfloat16)] * red_size,
            compiler_params=params(),
            cost_estimate=cost(4 * parts[0].size, 10 * parts[0].size),
        )(*parts, *deps)

    def send_plane(grads):
        return [grads[0], *(to_quarter(grads[r], r) for r in range(1, 4))]

    def send_line(parts):
        return [parts[0], *(shift_red(parts[s], s) for s in range(1, red_size))]

    def add_line(parts, *deps):
        shape = parts[0].shape
        kind = jnp.bfloat16 if dp_size <= 8 else jnp.float32
        owned = pl.pallas_call(
            ordered(functools.partial(line_kernel, red_size), 1 + red_size, len(deps)),
            grid=(1,),
            in_specs=[pl.BlockSpec(memory_space=pltpu.SMEM)]
            + [whole(shape)] * red_size
            + [ANY] * len(deps),
            out_specs=whole(shape),
            out_shape=jax.ShapeDtypeStruct(shape, kind),
            compiler_params=params(),
            cost_estimate=cost(8 * parts[0].size, 10 * parts[0].size),
        )(root.reshape(1), *parts, *deps)
        return other_groups(owned).astype(jnp.bfloat16)

    def spread(owned):
        return [owned, *(to_quarter(owned, r) for r in range(1, 4))]

    def place(chunk, mine, sib, grad_out):
        start, width = CHUNKS[chunk]
        near_column, columns = start // width, side // width
        has_out = 0 if grad_out is None else 1
        operands = [mine, sib] + ([grad_out] if has_out else [])
        return pl.pallas_call(
            functools.partial(place_kernel, has_out),
            grid_spec=pltpu.PrefetchScalarGridSpec(
                num_scalar_prefetch=1,
                grid=(2, 2),
                in_specs=[whole(mine.shape)] * 2 + [ANY] * has_out,
                out_specs=pl.BlockSpec(
                    (block, width),
                    lambda c, h, idx: (0, near_column + c * columns + h * 2 * columns),
                ),
            ),
            out_shape=jax.ShapeDtypeStruct((block, 2 * model_width), jnp.float32),
            input_output_aliases={3: 0} if has_out else {},
            compiler_params=params(),
            cost_estimate=cost(0, 20 * block * width),
        )(idx, *operands)

    outs, ghs, ws, sums = None, [], [], []
    on_way, planes, lines = [], [], []
    for chunk in range(n_chunks):
        deps = []
        if chunk == 0 and n_chunks > 1:
            deps += [packed[1][0], *firsts]
        if chunk + 1 < n_chunks and chunk > 0:
            packed.append(second_pack(z[chunk + 1], sums[-1]))
            near.append(second_sends(packed[-1]))
            deps += [packed[-1][0]]
        if chunk >= 2:
            planes.append(send_line(add_plane(on_way[chunk - 2], sums[-1])))
            deps += [planes[-1][0]]
        *outs, g0, g1, g2, g3, gh, w, tap_sums = middle(chunk, outs, deps)
        on_way.append(send_plane([g0, g1, g2, g3]))
        ghs.append(gh)
        ws.append(w)
        sums.append(tap_sums)

    out_other = to_core(outs[1])
    step = GROUP * length
    steps = own_rows // step
    row_spec = pl.BlockSpec((step, model_width), lambda i, *_: (i, 0))
    gh_specs = [pl.BlockSpec((step, gh.shape[1]), lambda i, *_: (i, 0)) for gh in ghs]
    sib_specs = [pl.BlockSpec((step, gh.shape[1]), lambda i, *_: (i + steps, 0)) for gh in ghs]
    w_specs = [whole(w.shape) for w in ws]
    flops = 2 * own_rows * model_width * model_width
    deps = [sums[-1]]
    while len(planes) < n_chunks - 1:
        planes.append(send_line(add_plane(on_way[len(planes)], sums[-1])))
        deps.append(planes[-1][0])
    while len(lines) < n_chunks - 2:
        lines.append(add_line(planes[len(lines)], sums[-1]))
        deps.append(lines[-1])
    grad_scaled_sib = pl.pallas_call(
        ordered(functools.partial(grad_scaled_kernel, n_chunks), 2 * n_chunks, len(deps)),
        grid=(steps,),
        in_specs=sib_specs + w_specs + [ANY] * len(deps),
        out_specs=row_spec,
        out_shape=jax.ShapeDtypeStruct((own_rows, model_width), jnp.bfloat16),
        compiler_params=params(),
        cost_estimate=cost(flops, 10 << 20),
    )(*ghs, *ws, *deps)
    other = to_core(grad_scaled_sib)
    deps = []
    while len(lines) < n_chunks - 1:
        lines.append(add_line(planes[len(lines)], grad_scaled_sib))
        deps.append(lines[-1])
    planes.append(send_line(add_plane(on_way[-1], grad_scaled_sib)))
    deps.append(planes[-1][0])
    side_spec = pl.BlockSpec((step, side), lambda i, *_: (i, 0))
    module_output, frame_gradient, gain_part = pl.pallas_call(
        ordered(functools.partial(frame_kernel, n_chunks), 8 + 2 * n_chunks, len(deps)),
        grid_spec=pltpu.PrefetchScalarGridSpec(
            num_scalar_prefetch=1,
            grid=(steps,),
            in_specs=[
                row_spec,
                row_spec,
                pl.BlockSpec((step, 128), lambda i, *_: (i, 0)),
                whole((1, model_width)),
                row_spec,
                side_spec,
                side_spec,
                *gh_specs,
                *w_specs,
                *[ANY] * len(deps),
            ],
            out_specs=[row_spec, row_spec, whole((8, model_width))],
        ),
        out_shape=[
            jax.ShapeDtypeStruct((own_rows, model_width), jnp.bfloat16),
            jax.ShapeDtypeStruct((own_rows, model_width), jnp.bfloat16),
            jax.ShapeDtypeStruct((8, model_width), jnp.float32),
        ],
        compiler_params=params(),
        cost_estimate=cost(2 * flops, 30 << 20),
    )(
        idx,
        flat_frames,
        flat_cot,
        live,
        gain.reshape(1, model_width),
        other,
        outs[0],
        out_other,
        *ghs,
        *ws,
        *deps,
    )

    while len(lines) < n_chunks:
        lines.append(add_line(planes[len(lines)], gain_part))
    grad_out = None
    for chunk in range(n_chunks):
        mine = jnp.stack(spread(lines[chunk]))
        grad_out = place(chunk, mine, to_core(mine), grad_out)

    order = sorted(range(n_chunks), key=lambda c: CHUNKS[c][0])
    tap_part = jnp.dot(
        back_matrix,
        jnp.concatenate([sums[c] for c in order], axis=1),
        precision=lax.Precision.HIGHEST,
    )
    gain_part = jnp.sum(gain_part, axis=0).reshape(2, side)
    kept = lax.dynamic_index_in_dim(gain_part, core, 0)
    sent = lax.dynamic_index_in_dim(gain_part, 1 - core, 0)
    small = jnp.concatenate([tap_part, kept + to_core(sent)], axis=0)
    small = tree_sum([small, *(to_quarter(small, r) for r in range(1, 4))])
    small = tree_sum([small, *(shift_red(small, s) for s in range(1, red_size))])
    small = other_groups(small) * root
    both = to_core(small)
    first = core == 0
    small = jnp.concatenate([jnp.where(first, small, both), jnp.where(first, both, small)], axis=1)
    return (
        module_output.reshape(frames.shape),
        frame_gradient.reshape(frames.shape),
        grad_out,
        small[:taps],
        small[taps],
    )


def solution(mesh):
    placed = (
        P(("dp", "red"), None, None),
        P(("dp", "red"), None, None),
        P("red", None),
        P(),
        P(),
        P(),
    )
    return jax.shard_map(
        local,
        mesh=mesh,
        in_specs=placed,
        out_specs=(
            P(("dp", "red"), None, None),
            P(("dp", "red"), None, None),
            P("red", None),
            P(),
            P(),
        ),
        check_vma=False,
    )
```

```python
import functools

import jax
import jax.numpy as jnp
import numpy as np
from jax import lax
from jax.experimental import pallas as pl
from jax.experimental.pallas import tpu as pltpu
from jax.sharding import PartitionSpec as P

EPSILON = 1e-05
GROUP = 4
VMEM_LIMIT = 48 * 1024 * 1024
CHUNKS = ((0, 256), (256, 256), (512, 256))


def split_bf16(x):
    high = x.astype(jnp.bfloat16)
    low = (x - high.astype(jnp.float32)).astype(jnp.bfloat16)
    return high, low


def time_transforms(length, taps):
    reach = taps // 2
    size = 16
    while size < length + reach:
        size *= 2
    half = size // 2
    f = np.arange(half)[:, None]
    t = np.arange(length)[None, :]
    angle = 2 * np.pi * f * t / size
    sign = np.where(np.arange(length) % 2 == 0, 1.0, -1.0)
    fwd_re, fwd_im = np.cos(angle), -np.sin(angle)
    fwd_im[0] = sign
    weight = np.where(np.arange(half) == 0, 1.0, 2.0)[:, None] / size
    inv_re, inv_im = (weight * np.cos(angle)).T, (-weight * np.sin(angle)).T
    inv_im[:, 0] = sign / size
    eye = np.eye(GROUP)
    forward = np.concatenate([np.kron(eye, fwd_re), np.kron(eye, fwd_im)], axis=0)
    inverse = np.concatenate([np.kron(eye, inv_re), np.kron(eye, inv_im)], axis=1)
    m = np.arange(taps) - reach
    tap_angle = 2 * np.pi * f * m[None, :] / size
    tap_sign = np.where(m % 2 == 0, 1.0, -1.0)
    hat_re, hat_im = np.cos(tap_angle), np.sin(tap_angle)
    hat_nyq = hat_re.copy()
    hat_nyq[0] = tap_sign
    hats = np.concatenate([hat_re, hat_im, hat_nyq], axis=0)
    back_1 = (weight * np.cos(tap_angle)).T
    back_2 = back_1.copy()
    back_2[:, 0] = tap_sign / size
    back_3 = (-weight * np.sin(tap_angle)).T
    back = np.concatenate([back_1, back_2, back_3], axis=1)
    return half, forward, inverse, hats.astype(np.float32), back.astype(np.float32)


def three_pass(matrix):
    high = matrix.astype(np.float32).astype(jnp.bfloat16)
    low = (matrix - high.astype(np.float64)).astype(np.float32).astype(jnp.bfloat16)
    return np.concatenate([high, low, high], axis=1)


def three_terms(x):
    high, low = split_bf16(x)
    return jnp.concatenate([high, high, low], axis=0)


def sigmoid(x):
    return 1.0 / (1.0 + jnp.exp(-x))


def scale_kernel(own, sib, gain, scaled, scaled_t):
    def run(frames):
        wide = frames[...].astype(jnp.float32)
        center = wide - jnp.mean(wide, axis=-1, keepdims=True)
        inv_std = lax.rsqrt(jnp.mean(center * center, axis=-1, keepdims=True) + EPSILON)
        res = (center * inv_std * gain[...]).astype(jnp.bfloat16)
        scaled[...] = res
        scaled_t[...] = res.T

    first = pl.program_id(0) < pl.num_programs(0) // 2
    pl.when(first)(lambda: run(own))
    pl.when(jnp.logical_not(first))(lambda: run(sib))


def chunk_kernel(red_size, length, start, has_out, idx, *rest):
    rest = list(rest)
    scaled_hbm, scaled_t_hbm, w_in = rest[:3]
    z_parts, rest = rest[3 : 2 + red_size], rest[2 + red_size :]
    xv, yg, frames_own, frames_sib, cot_own, cot_sib, live, hats, fwd, inv = rest[:10]
    rest = rest[10 + 2 * has_out :]
    outs_hbm, grads, gh_hbm, w_out, sums = rest[:2], rest[2:6], *rest[6:9]
    scaled, scaled_t, w, grad, out_own, out_sib, gh, sem_w, sem_s, sem_t, sem_o, sem_g = rest[9:]
    core, quarter, red, parity = idx[0], idx[1], idx[2], idx[3]
    n_rows, model_width = scaled.shape
    width = w.shape[1] // 2
    block = model_width // red_size
    half_block, part = block // 2, block // 4
    half = hats.shape[1]

    copies = []

    def fetch(src, row, rows, column):
        row = pl.multiple_of(row, 16)
        dst = w.at[pl.ds(row, rows), column : column + src.shape[-1]]
        copies.append(pltpu.make_async_copy(src, dst, sem_w.at[len(copies)]))

    for side in range(2):
        column = pl.multiple_of(core * (model_width // 2) + side * model_width + start, 128)
        fetch(w_in.at[:, pl.ds(column, width)], red * block, block, side * width)
    for s in range(1, red_size):
        row = lax.rem(red + red_size - s, red_size) * block
        fetch(z_parts[s - 1], row + parity * half_block, half_block, 0)
        fetch(xv.at[s - 1], row + (1 - parity) * half_block, half_block, 0)
        fetch(yg.at[s - 1], row + (1 - parity) * half_block, half_block, width)
    get_scaled = pltpu.make_async_copy(scaled_hbm, scaled, sem_s)
    get_scaled_t = pltpu.make_async_copy(scaled_t_hbm, scaled_t, sem_t)
    for copy in copies:
        copy.start()
    get_scaled.start()
    get_scaled_t.start()
    for copy in copies:
        copy.wait()
    near_columns = pl.ds(start, width)
    puts = [
        pltpu.make_async_copy(src, dst, sem_o.at[n])
        for n, (src, dst) in enumerate(
            (
                (w, w_out),
                (out_own, outs_hbm[0].at[:, near_columns]),
                (out_sib, outs_hbm[1].at[:, near_columns]),
                (gh, gh_hbm),
            )
        )
    ]
    puts[0].start()
    get_scaled.wait()

    rows = GROUP * length
    per_core = n_rows // rows // 2
    hat_a, hat_b, hat_c = hats[0], hats[1], hats[2]
    sums[...] = jnp.zeros_like(sums)

    def stages(group):
        at = pl.ds(group * rows, rows)
        local_at = pl.ds(group % per_core * rows, rows)
        if group < per_core:
            frames, cot, out = frames_own, cot_own, out_own
        else:
            frames, cot, out = frames_sib, cot_sib, out_sib

        def alive():
            return jnp.concatenate([live[at, :]] * (width // 128), axis=1)

        hidden = jnp.dot(scaled[at, :], w[...], preferred_element_type=jnp.float32)
        yield
        value = hidden[:, :width]
        gate = sigmoid(hidden[:, width:])
        terms = three_terms(value * gate * alive())
        yield
        x_hat = jnp.dot(fwd[...], terms, preferred_element_type=jnp.float32)
        yield
        x_hat = x_hat.reshape(2, GROUP, half, width)
        x_re, x_im = x_hat[0], x_hat[1]
        terms = three_terms(
            jnp.concatenate(
                [
                    (x_re * hat_a - x_im * hat_b).reshape(GROUP * half, width),
                    (x_re * hat_b + x_im * hat_c).reshape(GROUP * half, width),
                ],
                axis=0,
            )
        )
        yield
        conv = jnp.dot(inv[...], terms, preferred_element_type=jnp.float32)
        yield
        s = sigmoid(conv)
        wide = frames[local_at, :].astype(jnp.float32)
        out[local_at, :] = ((wide + conv * s) * alive()).astype(out.dtype)
        upstream = cot[local_at, :].astype(jnp.float32) * alive()
        terms = three_terms(upstream * (s * (1.0 + conv * (1.0 - s))))
        yield
        g_hat = jnp.dot(fwd[...], terms, preferred_element_type=jnp.float32)
        yield
        g_hat = g_hat.reshape(2, GROUP, half, width)
        g_re, g_im = g_hat[0], g_hat[1]
        sums[:half] += jnp.sum(g_re * x_re, axis=0)
        sums[half : 2 * half] += jnp.sum(g_im * x_im, axis=0)
        sums[2 * half :] += jnp.sum(g_re * x_im - g_im * x_re, axis=0)
        terms = three_terms(
            jnp.concatenate(
                [
                    (g_re * hat_a + g_im * hat_b).reshape(GROUP * half, width),
                    (g_im * hat_c - g_re * hat_b).reshape(GROUP * half, width),
                ],
                axis=0,
            )
        )
        yield
        grad_glu = jnp.dot(inv[...], terms, preferred_element_type=jnp.float32)
        yield
        grad_v = grad_glu * alive() * gate
        gh[at, :width] = grad_v.astype(jnp.bfloat16)
        gh[at, width:] = (grad_v * value * (1.0 - gate)).astype(jnp.bfloat16)

    running = [stages(group) for group in range(2 * per_core)]
    turn = 0
    while any(g is not None for g in running):
        for group in range(min(turn + 1, len(running))):
            if running[group] is not None:
                try:
                    next(running[group])
                except StopIteration:
                    running[group] = None
        turn += 1

    for put in puts[1:]:
        put.start()
    get_scaled_t.wait()
    sends = []
    for b in range(red_size):
        grad[pl.ds(b * block, block), :] = jnp.dot(
            scaled_t[pl.ds(b * block, block), :], gh[...], preferred_element_type=jnp.float32
        ).astype(jnp.bfloat16)
        for r in range(4):
            row = pl.multiple_of(b * block + lax.bitwise_xor(quarter, r) * part, 16)
            copy = pltpu.make_async_copy(
                grad.at[pl.ds(row, part), :], grads[r].at[b], sem_g.at[len(sends)]
            )
            copy.start()
            sends.append(copy)
    for copy in sends:
        copy.wait()
    for put in puts:
        put.wait()


def plane_kernel(*refs):
    out = refs[4]
    out[...] = tree_sum([p[...].astype(jnp.float32) for p in refs[:4]]).astype(out.dtype)


def grad_scaled_kernel(n_chunks, *refs):
    ghs, ws, out = refs[:n_chunks], refs[n_chunks : 2 * n_chunks], refs[2 * n_chunks]
    out[...] = scaled_gradient(ghs, ws).astype(out.dtype)


def scaled_gradient(ghs, ws):
    total = None
    for gh, w in zip(ghs, ws):
        term = lax.dot_general(
            gh[...], w[...], (((1,), (1,)), ((), ())), preferred_element_type=jnp.float32
        )
        total = term if total is None else total + term
    return total


def frame_kernel(n_chunks, idx, frames, cot, live, gain, other, out_mine, out_other, *rest):
    ghs, ws = rest[:n_chunks], rest[n_chunks : 2 * n_chunks]
    out, frame_out, gain_sum = rest[2 * n_chunks :]
    model_width = frames.shape[1]
    side = model_width // 2
    mine = pl.multiple_of(idx[0] * side, 128)
    out[:, pl.ds(mine, side)] = out_mine[...]
    out[:, pl.ds(pl.multiple_of(side - mine, 128), side)] = out_other[...]
    grad_scaled = scaled_gradient(ghs, ws) + other[...].astype(jnp.float32)
    wide = frames[...].astype(jnp.float32)
    center = wide - jnp.mean(wide, axis=-1, keepdims=True)
    inv_std = lax.rsqrt(jnp.mean(center * center, axis=-1, keepdims=True) + EPSILON)
    normed = center * inv_std
    part_sum = jnp.sum((grad_scaled * normed).reshape(-1, 8, model_width), axis=0)

    @pl.when(pl.program_id(0) == 0)
    def _():
        gain_sum[...] = part_sum

    @pl.when(pl.program_id(0) != 0)
    def _():
        gain_sum[...] += part_sum

    grad_normed = grad_scaled * gain[...]
    alive = jnp.concatenate([live[...]] * (model_width // 128), axis=1)
    upstream = cot[...].astype(jnp.float32) * alive
    res = upstream + inv_std * (
        grad_normed
        - jnp.mean(grad_normed, axis=-1, keepdims=True)
        - normed * jnp.mean(grad_normed * normed, axis=-1, keepdims=True)
    )
    frame_out[...] = (res * alive).astype(frame_out.dtype)


def stack_kernel(*refs):
    for r in range(4):
        refs[4][r] = refs[r][...]


def place_kernel(has_out, idx, mine, sib, *rest):
    out = rest[has_out]
    quarter = idx[1]
    part = mine.shape[2]
    chunk, which, side = pl.program_id(0), pl.program_id(1), pl.program_id(2)
    width = out.shape[1]

    def write(src):
        for r in range(4):
            q = lax.bitwise_xor(r, quarter)
            row = pl.ds(pl.multiple_of(q * part, 16), part)
            column = pl.ds(pl.multiple_of(side * width, 128), width)
            out[row, :] = src[r, chunk, :, column].astype(jnp.float32)

    own = which == idx[0]
    pl.when(own)(lambda: write(mine))
    pl.when(jnp.logical_not(own))(lambda: write(sib))


def pack_first_kernel(idx, values, gates, out):
    width = values.shape[1]
    out[:, :width] = values[...]
    out[:, width:] = gates[...]


def pack_second_kernel(n, *refs):
    parts, (out_v, out_g) = refs[:n], refs[n:]
    width = out_v.shape[2]
    for s in range(n):
        out_v[s] = parts[s][:, :width]
        out_g[s] = parts[s][:, width:]


def line_kernel(n, root, *refs):
    parts, out = refs[:n], refs[n]
    for k, part in enumerate(parts):
        terms = [part[b].astype(jnp.float32) for b in range(part.shape[0])]
        out[k] = (tree_sum(terms) * root[0]).astype(out.dtype)


def ordered(body, n_in, n_after):
    def kernel(*refs):
        return body(*refs[:n_in], *refs[n_in + n_after :])

    return kernel


def tree_sum(terms):
    if len(terms) == 1:
        return terms[0]
    return tree_sum(terms[::2]) + tree_sum(terms[1::2])


def whole(shape):
    return pl.BlockSpec(shape, lambda *_: (0,) * len(shape))


def params():
    return pltpu.CompilerParams(vmem_limit_bytes=VMEM_LIMIT)


LONG = pl.CostEstimate(flops=10**11, bytes_accessed=2 * 10**8, transcendentals=0)
SHORT = pl.CostEstimate(flops=10**6, bytes_accessed=10**6, transcendentals=0)


ANY = pl.BlockSpec(memory_space=pltpu.HBM)


def local(frames, cotangent, w_in, kernel, gain, lengths):
    dp_size = lax.axis_size("dp")
    red_size = lax.axis_size("red")
    dp = lax.axis_index("dp")
    red = lax.axis_index("red")
    local_utts, length, model_width = frames.shape
    taps = kernel.shape[0]
    block = model_width // red_size
    part = block // 4
    side = model_width // 2
    own_rows = local_utts * length
    n_rows = 2 * own_rows
    n_chunks = len(CHUNKS)

    core = dp % 2
    quarter = (dp // 2) % 4
    parity = (quarter + quarter // 2) % 2
    idx = jnp.stack([core, quarter, red, parity]).astype(jnp.int32)

    def to_core(x):
        return lax.ppermute(x, "dp", [(i, i ^ 1) for i in range(dp_size)])

    def to_quarter(x, r):
        return lax.ppermute(x, "dp", [(i, i ^ (2 * r)) for i in range(dp_size)])

    def shift_red(x, s):
        return lax.ppermute(x, "red", [(i, (i + s) % red_size) for i in range(red_size)])

    def other_groups(x):
        bit = 8
        while bit < dp_size:
            x = x + lax.ppermute(x, "dp", [(i, i ^ bit) for i in range(dp_size)])
            bit *= 2
        return x

    half, forward, inverse, hat_matrix, back_matrix = time_transforms(length, taps)
    fwd3, inv3 = jnp.asarray(three_pass(forward)), jnp.asarray(three_pass(inverse))

    flat_frames = frames.reshape(own_rows, model_width)
    flat_cot = cotangent.reshape(own_rows, model_width)

    def first_sends(chunk, *deps):
        start, width = CHUNKS[chunk]
        column, columns = start // width, side // width

        def strip(which):
            return pl.BlockSpec(
                (block // 2, width),
                lambda i, idx: (idx[3], idx[0] * columns + column + which * 2 * columns),
            )

        mine = pl.pallas_call(
            ordered(pack_first_kernel, 3, len(deps)),
            grid_spec=pltpu.PrefetchScalarGridSpec(
                num_scalar_prefetch=1,
                grid=(1,),
                in_specs=[strip(0), strip(1)] + [ANY] * len(deps),
                out_specs=whole((block // 2, 2 * width)),
            ),
            out_shape=jax.ShapeDtypeStruct((block // 2, 2 * width), jnp.bfloat16),
            compiler_params=params(),
            cost_estimate=LONG,
        )(idx, w_in, w_in, *deps)
        return mine, [shift_red(mine, s) for s in range(1, red_size)]

    def second_pack(z_parts, *deps):
        n = len(z_parts)
        width = z_parts[0].shape[1] // 2
        shape = (n, block // 2, width)
        return pl.pallas_call(
            ordered(functools.partial(pack_second_kernel, n), n, len(deps)),
            grid=(1,),
            in_specs=[whole(z_parts[0].shape)] * n + [ANY] * len(deps),
            out_specs=[whole(shape)] * 2,
            out_shape=[jax.ShapeDtypeStruct(shape, jnp.bfloat16)] * 2,
            compiler_params=params(),
            cost_estimate=LONG,
        )(*z_parts, *deps)

    def second_sends(packed):
        return to_quarter(packed[0], 1), to_quarter(packed[1], 2)

    mine, z_first = first_sends(0)
    z = [z_first]
    sib_frames, sib_cot = to_core(flat_frames), to_core(flat_cot)

    tile = 256
    tiles = own_rows // tile
    scaled, scaled_t = pl.pallas_call(
        ordered(scale_kernel, 3, 2),
        grid=(2 * tiles,),
        in_specs=[
            pl.BlockSpec((tile, model_width), lambda i: (jnp.minimum(i, tiles - 1), 0)),
            pl.BlockSpec((tile, model_width), lambda i: (jnp.maximum(i - tiles, 0), 0)),
            whole((1, model_width)),
            ANY,
            ANY,
        ],
        out_specs=[
            pl.BlockSpec((tile, model_width), lambda i: (i, 0)),
            pl.BlockSpec((model_width, tile), lambda i: (0, i)),
        ],
        out_shape=[
            pltpu.HBM((n_rows, model_width), jnp.bfloat16),
            pltpu.HBM((model_width, n_rows), jnp.bfloat16),
        ],
        compiler_params=params(),
        cost_estimate=LONG,
    )(flat_frames, sib_frames, gain.reshape(1, model_width), mine, sib_cot)

    packed = [second_pack(z[0], scaled)]
    near = [second_sends(packed[0])]
    firsts = []
    for chunk in range(1, n_chunks):
        mine, z_next = first_sends(chunk, *z[-1], *([scaled] if chunk == 1 else []))
        z.append(z_next)
        firsts.append(mine)
    if n_chunks > 1:
        packed.append(second_pack(z[1], *near[0]))
        near.append(second_sends(packed[1]))

    by_owner = lengths.reshape(dp_size, red_size, local_utts)

    def alive_rows(device):
        own = lax.dynamic_slice(by_owner, (device, red, 0), (1, 1, local_utts)).reshape(local_utts)
        return jnp.arange(length, dtype=jnp.int32)[None, :] < own[:, None]

    alive = jnp.stack([alive_rows(dp), alive_rows(dp + 1 - 2 * core)]).astype(jnp.float32)
    live = jnp.broadcast_to(alive.reshape(n_rows, 1), (n_rows, 128))
    root = lax.rsqrt(jnp.sum(lengths).astype(jnp.float32))
    hats = jnp.dot(hat_matrix, kernel, precision=lax.Precision.HIGHEST).reshape(3, half, model_width)

    def middle(chunk, outs, deps):
        start, width = CHUNKS[chunk]
        near_column = start // width
        columns = side // width

        def strip(*leading):
            return pl.BlockSpec(
                (*leading, width),
                lambda i, idx: (*(0 for _ in leading), idx[0] * columns + near_column),
            )

        operands = [scaled, scaled_t, w_in, *z[chunk], *near[chunk]]
        in_specs = [ANY] * len(operands)
        operands += [flat_frames, sib_frames, flat_cot, sib_cot, live, hats, fwd3, inv3]
        in_specs += [strip(own_rows)] * 4
        in_specs += [whole((n_rows, 128)), strip(3, half), whole(fwd3.shape), whole(inv3.shape)]
        aliases = {}
        if outs is not None:
            aliases = {len(operands) + 1: 0, len(operands) + 2: 1}
            operands += outs
            in_specs += [ANY] * 2
        n_in = len(operands) + 1
        operands += deps
        in_specs += [ANY] * len(deps)
        return pl.pallas_call(
            ordered(
                functools.partial(chunk_kernel, red_size, length, start, 1 if aliases else 0),
                n_in,
                len(deps),
            ),
            grid_spec=pltpu.PrefetchScalarGridSpec(
                num_scalar_prefetch=1,
                grid=(1,),
                in_specs=in_specs,
                out_specs=[ANY] * 8 + [whole((3 * half, width))],
                scratch_shapes=[
                    pltpu.VMEM((n_rows, model_width), jnp.bfloat16),
                    pltpu.VMEM((model_width, n_rows), jnp.bfloat16),
                    pltpu.VMEM((model_width, 2 * width), jnp.bfloat16),
                    pltpu.VMEM((model_width, 2 * width), jnp.bfloat16),
                    pltpu.VMEM((own_rows, width), jnp.bfloat16),
                    pltpu.VMEM((own_rows, width), jnp.bfloat16),
                    pltpu.VMEM((n_rows, 2 * width), jnp.bfloat16),
                    pltpu.SemaphoreType.DMA((3 * red_size - 1,)),
                    pltpu.SemaphoreType.DMA,
                    pltpu.SemaphoreType.DMA,
                    pltpu.SemaphoreType.DMA((4,)),
                    pltpu.SemaphoreType.DMA((4 * red_size,)),
                ],
            ),
            out_shape=[
                pltpu.HBM((own_rows, side), jnp.bfloat16),
                pltpu.HBM((own_rows, side), jnp.bfloat16),
                *[jax.ShapeDtypeStruct((red_size, part, 2 * width), jnp.bfloat16)] * 4,
                pltpu.HBM((n_rows, 2 * width), jnp.bfloat16),
                jax.ShapeDtypeStruct((model_width, 2 * width), jnp.bfloat16),
                jax.ShapeDtypeStruct((3 * half, width), jnp.float32),
            ],
            input_output_aliases=aliases,
            compiler_params=params(),
            cost_estimate=LONG,
        )(idx, *operands)

    def add_plane(parts, *deps):
        shape = parts[0].shape
        return pl.pallas_call(
            ordered(plane_kernel, 4, len(deps)),
            grid=(1,),
            in_specs=[whole(shape)] * 4 + [ANY] * len(deps),
            out_specs=whole(shape),
            out_shape=jax.ShapeDtypeStruct(shape, jnp.bfloat16),
            compiler_params=params(),
            cost_estimate=LONG,
        )(*parts, *deps)

    def send_plane(grads):
        return [grads[0], *(to_quarter(grads[r], r) for r in range(1, 4))]

    def send_line(parts):
        return lax.all_to_all(parts, "red", 0, 0, tiled=True)

    def add_line(parts, *deps):
        shape = parts[0].shape
        out_shape = (len(parts), *shape[1:])
        kind = jnp.bfloat16 if dp_size <= 8 else jnp.float32
        owned = pl.pallas_call(
            ordered(functools.partial(line_kernel, len(parts)), 1 + len(parts), len(deps)),
            grid=(1,),
            in_specs=[pl.BlockSpec(memory_space=pltpu.SMEM)]
            + [whole(shape)] * len(parts)
            + [ANY] * len(deps),
            out_specs=whole(out_shape),
            out_shape=jax.ShapeDtypeStruct(out_shape, kind),
            compiler_params=params(),
            cost_estimate=LONG,
        )(root.reshape(1), *parts, *deps)
        return other_groups(owned).astype(jnp.bfloat16)

    def spread(owned, *deps):
        parts = [owned, *(to_quarter(owned, r) for r in range(1, 4))]
        return pl.pallas_call(
            ordered(stack_kernel, 4, len(deps)),
            grid=(1,),
            in_specs=[whole(owned.shape)] * 4 + [ANY] * len(deps),
            out_specs=whole((4, *owned.shape)),
            out_shape=jax.ShapeDtypeStruct((4, *owned.shape), owned.dtype),
            compiler_params=params(),
            cost_estimate=SHORT,
        )(*parts, *deps)

    def place(first, mine, sib, grad_out, estimate):
        start, width = CHUNKS[first]
        near_column, columns = start // width, side // width
        has_out = 0 if grad_out is None else 1
        operands = [mine, sib] + ([grad_out] if has_out else [])
        return pl.pallas_call(
            functools.partial(place_kernel, has_out),
            grid_spec=pltpu.PrefetchScalarGridSpec(
                num_scalar_prefetch=1,
                grid=(mine.shape[1], 2, 2),
                in_specs=[whole(mine.shape)] * 2 + [ANY] * has_out,
                out_specs=pl.BlockSpec(
                    (block, width),
                    lambda k, c, h, idx: (0, near_column + k + c * columns + h * 2 * columns),
                ),
            ),
            out_shape=jax.ShapeDtypeStruct((block, 2 * model_width), jnp.float32),
            input_output_aliases={3: 0} if has_out else {},
            compiler_params=params(),
            cost_estimate=estimate,
        )(idx, *operands)

    outs, ghs, ws, sums = None, [], [], []
    on_way, planes, after_plane = [], [], []

    def step_plane(chunk, *deps):
        after_plane.append(add_plane(on_way[chunk], *deps))
        planes.append(send_line(after_plane[-1]))

    for chunk in range(n_chunks):
        deps = []
        if chunk == 0 and n_chunks > 1:
            deps += [packed[1][0], *firsts]
        if chunk + 1 < n_chunks and chunk > 0:
            packed.append(second_pack(z[chunk + 1], sums[-1]))
            near.append(second_sends(packed[-1]))
            deps += [packed[-1][0]]
        if chunk >= 2:
            step_plane(chunk - 2, sums[-1])
            deps += [after_plane[-1]]
        *outs, g0, g1, g2, g3, gh, w, tap_sums = middle(chunk, outs, deps)
        on_way.append(send_plane([g0, g1, g2, g3]))
        ghs.append(gh)
        ws.append(w)
        sums.append(tap_sums)

    out_other = to_core(outs[1])
    step = own_rows // 2
    steps = own_rows // step
    row_spec = pl.BlockSpec((step, model_width), lambda i, *_: (i, 0))
    gh_specs = [pl.BlockSpec((step, gh.shape[1]), lambda i, *_: (i, 0)) for gh in ghs]
    sib_specs = [pl.BlockSpec((step, gh.shape[1]), lambda i, *_: (i + steps, 0)) for gh in ghs]
    w_specs = [whole(w.shape) for w in ws]
    flops = 2 * own_rows * model_width * model_width
    deps = [sums[-1]]
    while len(planes) < n_chunks - 1:
        step_plane(len(planes), sums[-1])
        deps.append(after_plane[-1])
    grad_scaled_sib = pl.pallas_call(
        ordered(functools.partial(grad_scaled_kernel, n_chunks), 2 * n_chunks, len(deps)),
        grid=(1,),
        in_specs=[pl.BlockSpec((own_rows, gh.shape[1]), lambda i: (1, 0)) for gh in ghs]
        + w_specs
        + [ANY] * len(deps),
        out_specs=whole((own_rows, model_width)),
        out_shape=jax.ShapeDtypeStruct((own_rows, model_width), jnp.bfloat16),
        compiler_params=params(),
        cost_estimate=LONG,
    )(*ghs, *ws, *deps)
    other = to_core(grad_scaled_sib)
    early = add_line(planes, grad_scaled_sib)
    step_plane(n_chunks - 1, early)
    deps = [after_plane[-1]]
    side_spec = pl.BlockSpec((step, side), lambda i, *_: (i, 0))
    module_output, frame_gradient, gain_part = pl.pallas_call(
        ordered(functools.partial(frame_kernel, n_chunks), 8 + 2 * n_chunks, len(deps)),
        grid_spec=pltpu.PrefetchScalarGridSpec(
            num_scalar_prefetch=1,
            grid=(steps,),
            in_specs=[
                row_spec,
                row_spec,
                pl.BlockSpec((step, 128), lambda i, *_: (i, 0)),
                whole((1, model_width)),
                row_spec,
                side_spec,
                side_spec,
                *gh_specs,
                *w_specs,
                *[ANY] * len(deps),
            ],
            out_specs=[row_spec, row_spec, whole((8, model_width))],
        ),
        out_shape=[
            jax.ShapeDtypeStruct((own_rows, model_width), jnp.bfloat16),
            jax.ShapeDtypeStruct((own_rows, model_width), jnp.bfloat16),
            jax.ShapeDtypeStruct((8, model_width), jnp.float32),
        ],
        compiler_params=params(),
        cost_estimate=LONG,
    )(
        idx,
        flat_frames,
        flat_cot,
        live,
        gain.reshape(1, model_width),
        other,
        outs[0],
        out_other,
        *ghs,
        *ws,
        *deps,
    )

    mine = spread(early)
    grad_out = place(0, mine, to_core(mine), None, LONG)
    mine = spread(add_line(planes[-1:]), grad_out)
    grad_out = place(n_chunks - 1, mine, to_core(mine), grad_out, SHORT)

    order = sorted(range(n_chunks), key=lambda c: CHUNKS[c][0])
    tap_part = jnp.dot(
        back_matrix,
        jnp.concatenate([sums[c] for c in order], axis=1),
        precision=lax.Precision.HIGHEST,
    )
    gain_part = jnp.sum(gain_part, axis=0).reshape(2, side)
    small = jnp.concatenate([tap_part, gain_part], axis=0)
    for r in (1, 2):
        small = small + to_quarter(small, r)
    bit = 1
    while bit < red_size:
        small = small + lax.ppermute(small, "red", [(i, i ^ bit) for i in range(red_size)])
        bit *= 2
    small = other_groups(small) * root
    both = to_core(small)
    first = core == 0
    left, right = jnp.where(first, small, both), jnp.where(first, both, small)
    tap_total = jnp.concatenate([left[:taps], right[:taps]], axis=1)
    gain_total = (small[taps:] + both[taps:]).reshape(model_width)
    return (
        module_output.reshape(frames.shape),
        frame_gradient.reshape(frames.shape),
        grad_out,
        tap_total,
        gain_total,
    )


def solution(mesh):
    placed = (
        P(("dp", "red"), None, None),
        P(("dp", "red"), None, None),
        P("red", None),
        P(),
        P(),
        P(),
    )
    return jax.shard_map(
        local,
        mesh=mesh,
        in_specs=placed,
        out_specs=(
            P(("dp", "red"), None, None),
            P(("dp", "red"), None, None),
            P("red", None),
            P(),
            P(),
        ),
        check_vma=False,
    )
```

```python
import functools

import jax
import jax.numpy as jnp
import numpy as np
from jax import lax
from jax.experimental import pallas as pl
from jax.experimental.pallas import tpu as pltpu
from jax.sharding import PartitionSpec as P

EPSILON = 1e-05
GROUP = 4
VMEM_LIMIT = 48 * 1024 * 1024
CHUNKS = ((0, 256), (256, 256), (512, 256))


def split_bf16(x):
    high = x.astype(jnp.bfloat16)
    low = (x - high.astype(jnp.float32)).astype(jnp.bfloat16)
    return high, low


def time_transforms(length, taps):
    reach = taps // 2
    size = 16
    while size < length + reach:
        size *= 2
    half = size // 2
    f = np.arange(half)[:, None]
    t = np.arange(length)[None, :]
    angle = 2 * np.pi * f * t / size
    sign = np.where(np.arange(length) % 2 == 0, 1.0, -1.0)
    fwd_re, fwd_im = np.cos(angle), -np.sin(angle)
    fwd_im[0] = sign
    weight = np.where(np.arange(half) == 0, 1.0, 2.0)[:, None] / size
    inv_re, inv_im = (weight * np.cos(angle)).T, (-weight * np.sin(angle)).T
    inv_im[:, 0] = sign / size
    eye = np.eye(GROUP)
    forward = np.concatenate([np.kron(eye, fwd_re), np.kron(eye, fwd_im)], axis=0)
    inverse = np.concatenate([np.kron(eye, inv_re), np.kron(eye, inv_im)], axis=1)
    m = np.arange(taps) - reach
    tap_angle = 2 * np.pi * f * m[None, :] / size
    tap_sign = np.where(m % 2 == 0, 1.0, -1.0)
    hat_re, hat_im = np.cos(tap_angle), np.sin(tap_angle)
    hat_nyq = hat_re.copy()
    hat_nyq[0] = tap_sign
    hats = np.concatenate([hat_re, hat_im, hat_nyq], axis=0)
    back_1 = (weight * np.cos(tap_angle)).T
    back_2 = back_1.copy()
    back_2[:, 0] = tap_sign / size
    back_3 = (-weight * np.sin(tap_angle)).T
    back = np.concatenate([back_1, back_2, back_3], axis=1)
    return half, forward, inverse, hats.astype(np.float32), back.astype(np.float32)


def three_pass(matrix):
    high = matrix.astype(np.float32).astype(jnp.bfloat16)
    low = (matrix - high.astype(np.float64)).astype(np.float32).astype(jnp.bfloat16)
    return np.concatenate([high, low, high], axis=1)


def three_terms(x):
    high, low = split_bf16(x)
    return jnp.concatenate([high, high, low], axis=0)


def sigmoid(x):
    return 1.0 / (1.0 + jnp.exp(-x))


def scale_kernel(own, sib, gain, scaled, scaled_t):
    def run(frames):
        wide = frames[...].astype(jnp.float32)
        center = wide - jnp.mean(wide, axis=-1, keepdims=True)
        inv_std = lax.rsqrt(jnp.mean(center * center, axis=-1, keepdims=True) + EPSILON)
        res = (center * inv_std * gain[...]).astype(jnp.bfloat16)
        scaled[...] = res
        scaled_t[...] = res.T

    first = pl.program_id(0) < pl.num_programs(0) // 2
    pl.when(first)(lambda: run(own))
    pl.when(jnp.logical_not(first))(lambda: run(sib))


def chunk_kernel(red_size, length, start, has_out, idx, *rest):
    rest = list(rest)
    scaled_hbm, scaled_t_hbm, w_in = rest[:3]
    z_parts, rest = rest[3 : 2 + red_size], rest[2 + red_size :]
    xv, yg, frames_own, frames_sib, cot_own, cot_sib, live, hats, fwd, inv = rest[:10]
    rest = rest[10 + 2 * has_out :]
    outs_hbm, grads, gh_hbm, w_out, sums = rest[:2], rest[2:6], *rest[6:9]
    scaled, scaled_t, w, grad, out_own, out_sib, gh, sem_w, sem_s, sem_t, sem_o, sem_g = rest[9:]
    core, quarter, red, parity = idx[0], idx[1], idx[2], idx[3]
    n_rows, model_width = scaled.shape
    width = w.shape[1] // 2
    block = model_width // red_size
    half_block, part = block // 2, block // 4
    half = hats.shape[1]

    copies = []

    def fetch(src, row, rows, column):
        row = pl.multiple_of(row, 16)
        dst = w.at[pl.ds(row, rows), column : column + src.shape[-1]]
        copies.append(pltpu.make_async_copy(src, dst, sem_w.at[len(copies)]))

    for side in range(2):
        column = pl.multiple_of(core * (model_width // 2) + side * model_width + start, 128)
        fetch(w_in.at[:, pl.ds(column, width)], red * block, block, side * width)
    for s in range(1, red_size):
        row = lax.rem(red + red_size - s, red_size) * block
        fetch(z_parts[s - 1], row + parity * half_block, half_block, 0)
        fetch(xv.at[s - 1], row + (1 - parity) * half_block, half_block, 0)
        fetch(yg.at[s - 1], row + (1 - parity) * half_block, half_block, width)
    get_scaled = pltpu.make_async_copy(scaled_hbm, scaled, sem_s)
    get_scaled_t = pltpu.make_async_copy(scaled_t_hbm, scaled_t, sem_t)
    for copy in copies:
        copy.start()
    get_scaled.start()
    get_scaled_t.start()
    for copy in copies:
        copy.wait()
    near_columns = pl.ds(start, width)
    puts = [
        pltpu.make_async_copy(src, dst, sem_o.at[n])
        for n, (src, dst) in enumerate(
            (
                (w, w_out),
                (out_own, outs_hbm[0].at[:, near_columns]),
                (out_sib, outs_hbm[1].at[:, near_columns]),
                (gh, gh_hbm),
            )
        )
    ]
    puts[0].start()
    get_scaled.wait()

    rows = GROUP * length
    per_core = n_rows // rows // 2
    hat_a, hat_b, hat_c = hats[0], hats[1], hats[2]
    sums[...] = jnp.zeros_like(sums)

    def stages(group):
        at = pl.ds(group * rows, rows)
        local_at = pl.ds(group % per_core * rows, rows)
        if group < per_core:
            frames, cot, out = frames_own, cot_own, out_own
        else:
            frames, cot, out = frames_sib, cot_sib, out_sib

        def alive():
            return jnp.concatenate([live[at, :]] * (width // 128), axis=1)

        hidden = jnp.dot(scaled[at, :], w[...], preferred_element_type=jnp.float32)
        yield
        value = hidden[:, :width]
        gate = sigmoid(hidden[:, width:])
        terms = three_terms(value * gate * alive())
        yield
        x_hat = jnp.dot(fwd[...], terms, preferred_element_type=jnp.float32)
        yield
        x_hat = x_hat.reshape(2, GROUP, half, width)
        x_re, x_im = x_hat[0], x_hat[1]
        terms = three_terms(
            jnp.concatenate(
                [
                    (x_re * hat_a - x_im * hat_b).reshape(GROUP * half, width),
                    (x_re * hat_b + x_im * hat_c).reshape(GROUP * half, width),
                ],
                axis=0,
            )
        )
        yield
        conv = jnp.dot(inv[...], terms, preferred_element_type=jnp.float32)
        yield
        s = sigmoid(conv)
        wide = frames[local_at, :].astype(jnp.float32)
        out[local_at, :] = ((wide + conv * s) * alive()).astype(out.dtype)
        upstream = cot[local_at, :].astype(jnp.float32) * alive()
        terms = three_terms(upstream * (s * (1.0 + conv * (1.0 - s))))
        yield
        g_hat = jnp.dot(fwd[...], terms, preferred_element_type=jnp.float32)
        yield
        g_hat = g_hat.reshape(2, GROUP, half, width)
        g_re, g_im = g_hat[0], g_hat[1]
        sums[:half] += jnp.sum(g_re * x_re, axis=0)
        sums[half : 2 * half] += jnp.sum(g_im * x_im, axis=0)
        sums[2 * half :] += jnp.sum(g_re * x_im - g_im * x_re, axis=0)
        terms = three_terms(
            jnp.concatenate(
                [
                    (g_re * hat_a + g_im * hat_b).reshape(GROUP * half, width),
                    (g_im * hat_c - g_re * hat_b).reshape(GROUP * half, width),
                ],
                axis=0,
            )
        )
        yield
        grad_glu = jnp.dot(inv[...], terms, preferred_element_type=jnp.float32)
        yield
        grad_v = grad_glu * alive() * gate
        gh[at, :width] = grad_v.astype(jnp.bfloat16)
        gh[at, width:] = (grad_v * value * (1.0 - gate)).astype(jnp.bfloat16)

    running = [stages(group) for group in range(2 * per_core)]
    turn = 0
    while any(g is not None for g in running):
        for group in range(min(turn + 1, len(running))):
            if running[group] is not None:
                try:
                    next(running[group])
                except StopIteration:
                    running[group] = None
        turn += 1

    for put in puts[1:]:
        put.start()
    get_scaled_t.wait()
    sends = []
    for b in range(red_size):
        grad[pl.ds(b * block, block), :] = jnp.dot(
            scaled_t[pl.ds(b * block, block), :], gh[...], preferred_element_type=jnp.float32
        ).astype(jnp.bfloat16)
        for r in range(4):
            row = pl.multiple_of(b * block + lax.bitwise_xor(quarter, r) * part, 16)
            copy = pltpu.make_async_copy(
                grad.at[pl.ds(row, part), :], grads[r].at[b], sem_g.at[len(sends)]
            )
            copy.start()
            sends.append(copy)
    for copy in sends:
        copy.wait()
    for put in puts:
        put.wait()


def plane_kernel(*refs):
    out = refs[4]
    out[...] = tree_sum([p[...].astype(jnp.float32) for p in refs[:4]]).astype(out.dtype)


def grad_scaled_kernel(n_chunks, *refs):
    ghs, ws, out = refs[:n_chunks], refs[n_chunks : 2 * n_chunks], refs[2 * n_chunks]
    out[...] = scaled_gradient(ghs, ws).astype(out.dtype)


def scaled_gradient(ghs, ws):
    total = None
    for gh, w in zip(ghs, ws):
        term = lax.dot_general(
            gh[...], w[...], (((1,), (1,)), ((), ())), preferred_element_type=jnp.float32
        )
        total = term if total is None else total + term
    return total


def frame_kernel(n_chunks, idx, frames, cot, live, gain, other, out_mine, out_other, *rest):
    ghs, ws = rest[:n_chunks], rest[n_chunks : 2 * n_chunks]
    out, frame_out, gain_sum = rest[2 * n_chunks :]
    model_width = frames.shape[1]
    side = model_width // 2
    mine = pl.multiple_of(idx[0] * side, 128)
    out[:, pl.ds(mine, side)] = out_mine[...]
    out[:, pl.ds(pl.multiple_of(side - mine, 128), side)] = out_other[...]
    grad_scaled = scaled_gradient(ghs, ws) + other[...].astype(jnp.float32)
    wide = frames[...].astype(jnp.float32)
    center = wide - jnp.mean(wide, axis=-1, keepdims=True)
    inv_std = lax.rsqrt(jnp.mean(center * center, axis=-1, keepdims=True) + EPSILON)
    normed = center * inv_std
    part_sum = jnp.sum((grad_scaled * normed).reshape(-1, 8, model_width), axis=0)

    @pl.when(pl.program_id(0) == 0)
    def _():
        gain_sum[...] = part_sum

    @pl.when(pl.program_id(0) != 0)
    def _():
        gain_sum[...] += part_sum

    grad_normed = grad_scaled * gain[...]
    alive = jnp.concatenate([live[...]] * (model_width // 128), axis=1)
    upstream = cot[...].astype(jnp.float32) * alive
    res = upstream + inv_std * (
        grad_normed
        - jnp.mean(grad_normed, axis=-1, keepdims=True)
        - normed * jnp.mean(grad_normed * normed, axis=-1, keepdims=True)
    )
    frame_out[...] = (res * alive).astype(frame_out.dtype)


def stack_kernel(*refs):
    for r in range(4):
        refs[4][r] = refs[r][...]


def place_kernel(has_out, idx, mine, sib, *rest):
    out = rest[has_out]
    quarter = idx[1]
    part = mine.shape[2]
    chunk, which, side = pl.program_id(0), pl.program_id(1), pl.program_id(2)
    width = out.shape[1]

    def write(src):
        for r in range(4):
            q = lax.bitwise_xor(r, quarter)
            row = pl.ds(pl.multiple_of(q * part, 16), part)
            column = pl.ds(pl.multiple_of(side * width, 128), width)
            out[row, :] = src[r, chunk, :, column].astype(jnp.float32)

    own = which == idx[0]
    pl.when(own)(lambda: write(mine))
    pl.when(jnp.logical_not(own))(lambda: write(sib))


def pack_first_kernel(idx, values, gates, out):
    width = values.shape[1]
    out[:, :width] = values[...]
    out[:, width:] = gates[...]


def pack_second_kernel(n, *refs):
    parts, (out_v, out_g) = refs[:n], refs[n:]
    width = out_v.shape[2]
    for s in range(n):
        out_v[s] = parts[s][:, :width]
        out_g[s] = parts[s][:, width:]


def line_kernel(n, root, *refs):
    parts, out = refs[:n], refs[n]
    for k, part in enumerate(parts):
        terms = [part[b].astype(jnp.float32) for b in range(part.shape[0])]
        out[k] = (tree_sum(terms) * root[0]).astype(out.dtype)


def ordered(body, n_in, n_after):
    def kernel(*refs):
        return body(*refs[:n_in], *refs[n_in + n_after :])

    return kernel


def tree_sum(terms):
    if len(terms) == 1:
        return terms[0]
    return tree_sum(terms[::2]) + tree_sum(terms[1::2])


def whole(shape):
    return pl.BlockSpec(shape, lambda *_: (0,) * len(shape))


def params():
    return pltpu.CompilerParams(vmem_limit_bytes=VMEM_LIMIT)


LONG = pl.CostEstimate(flops=10**11, bytes_accessed=2 * 10**8, transcendentals=0)
SHORT = pl.CostEstimate(flops=10**6, bytes_accessed=10**6, transcendentals=0)


ANY = pl.BlockSpec(memory_space=pltpu.HBM)


def local(frames, cotangent, w_in, kernel, gain, lengths):
    dp_size = lax.axis_size("dp")
    red_size = lax.axis_size("red")
    dp = lax.axis_index("dp")
    red = lax.axis_index("red")
    local_utts, length, model_width = frames.shape
    taps = kernel.shape[0]
    block = model_width // red_size
    part = block // 4
    side = model_width // 2
    own_rows = local_utts * length
    n_rows = 2 * own_rows
    n_chunks = len(CHUNKS)

    core = dp % 2
    quarter = (dp // 2) % 4
    parity = (quarter + quarter // 2) % 2
    idx = jnp.stack([core, quarter, red, parity]).astype(jnp.int32)

    def to_core(x):
        return lax.ppermute(x, "dp", [(i, i ^ 1) for i in range(dp_size)])

    def to_quarter(x, r):
        return lax.ppermute(x, "dp", [(i, i ^ (2 * r)) for i in range(dp_size)])

    def shift_red(x, s):
        return lax.ppermute(x, "red", [(i, (i + s) % red_size) for i in range(red_size)])

    def other_groups(x):
        bit = 8
        while bit < dp_size:
            x = x + lax.ppermute(x, "dp", [(i, i ^ bit) for i in range(dp_size)])
            bit *= 2
        return x

    half, forward, inverse, hat_matrix, back_matrix = time_transforms(length, taps)
    fwd3, inv3 = jnp.asarray(three_pass(forward)), jnp.asarray(three_pass(inverse))

    flat_frames = frames.reshape(own_rows, model_width)
    flat_cot = cotangent.reshape(own_rows, model_width)

    def first_sends(chunk, *deps):
        start, width = CHUNKS[chunk]
        column, columns = start // width, side // width

        def strip(which):
            return pl.BlockSpec(
                (block // 2, width),
                lambda i, idx: (idx[3], idx[0] * columns + column + which * 2 * columns),
            )

        mine = pl.pallas_call(
            ordered(pack_first_kernel, 3, len(deps)),
            grid_spec=pltpu.PrefetchScalarGridSpec(
                num_scalar_prefetch=1,
                grid=(1,),
                in_specs=[strip(0), strip(1)] + [ANY] * len(deps),
                out_specs=whole((block // 2, 2 * width)),
            ),
            out_shape=jax.ShapeDtypeStruct((block // 2, 2 * width), jnp.bfloat16),
            compiler_params=params(),
            cost_estimate=LONG,
        )(idx, w_in, w_in, *deps)
        return mine, [shift_red(mine, s) for s in range(1, red_size)]

    def second_pack(z_parts, *deps):
        n = len(z_parts)
        width = z_parts[0].shape[1] // 2
        shape = (n, block // 2, width)
        return pl.pallas_call(
            ordered(functools.partial(pack_second_kernel, n), n, len(deps)),
            grid=(1,),
            in_specs=[whole(z_parts[0].shape)] * n + [ANY] * len(deps),
            out_specs=[whole(shape)] * 2,
            out_shape=[jax.ShapeDtypeStruct(shape, jnp.bfloat16)] * 2,
            compiler_params=params(),
            cost_estimate=LONG,
        )(*z_parts, *deps)

    def second_sends(packed):
        return to_quarter(packed[0], 1), to_quarter(packed[1], 2)

    mine, z_first = first_sends(0)
    z = [z_first]
    sib_frames, sib_cot = to_core(flat_frames), to_core(flat_cot)

    tile = 256
    tiles = own_rows // tile
    scaled, scaled_t = pl.pallas_call(
        ordered(scale_kernel, 3, 2),
        grid=(2 * tiles,),
        in_specs=[
            pl.BlockSpec((tile, model_width), lambda i: (jnp.minimum(i, tiles - 1), 0)),
            pl.BlockSpec((tile, model_width), lambda i: (jnp.maximum(i - tiles, 0), 0)),
            whole((1, model_width)),
            ANY,
            ANY,
        ],
        out_specs=[
            pl.BlockSpec((tile, model_width), lambda i: (i, 0)),
            pl.BlockSpec((model_width, tile), lambda i: (0, i)),
        ],
        out_shape=[
            pltpu.HBM((n_rows, model_width), jnp.bfloat16),
            pltpu.HBM((model_width, n_rows), jnp.bfloat16),
        ],
        compiler_params=params(),
        cost_estimate=LONG,
    )(flat_frames, sib_frames, gain.reshape(1, model_width), mine, sib_cot)

    packed = [second_pack(z[0], scaled)]
    near = [second_sends(packed[0])]
    firsts = []
    for chunk in range(1, n_chunks):
        mine, z_next = first_sends(chunk, *z[-1], *([scaled] if chunk == 1 else []))
        z.append(z_next)
        firsts.append(mine)
    if n_chunks > 1:
        packed.append(second_pack(z[1], *near[0]))
        near.append(second_sends(packed[1]))

    by_owner = lengths.reshape(dp_size, red_size, local_utts)

    def alive_rows(device):
        own = lax.dynamic_slice(by_owner, (device, red, 0), (1, 1, local_utts)).reshape(local_utts)
        return jnp.arange(length, dtype=jnp.int32)[None, :] < own[:, None]

    alive = jnp.stack([alive_rows(dp), alive_rows(dp + 1 - 2 * core)]).astype(jnp.float32)
    live = jnp.broadcast_to(alive.reshape(n_rows, 1), (n_rows, 128))
    root = lax.rsqrt(jnp.sum(lengths).astype(jnp.float32))
    hats = jnp.dot(hat_matrix, kernel, precision=lax.Precision.HIGHEST).reshape(3, half, model_width)

    def middle(chunk, outs, deps):
        start, width = CHUNKS[chunk]
        near_column = start // width
        columns = side // width

        def strip(*leading):
            return pl.BlockSpec(
                (*leading, width),
                lambda i, idx: (*(0 for _ in leading), idx[0] * columns + near_column),
            )

        operands = [scaled, scaled_t, w_in, *z[chunk], *near[chunk]]
        in_specs = [ANY] * len(operands)
        operands += [flat_frames, sib_frames, flat_cot, sib_cot, live, hats, fwd3, inv3]
        in_specs += [strip(own_rows)] * 4
        in_specs += [whole((n_rows, 128)), strip(3, half), whole(fwd3.shape), whole(inv3.shape)]
        aliases = {}
        if outs is not None:
            aliases = {len(operands) + 1: 0, len(operands) + 2: 1}
            operands += outs
            in_specs += [ANY] * 2
        n_in = len(operands) + 1
        operands += deps
        in_specs += [ANY] * len(deps)
        return pl.pallas_call(
            ordered(
                functools.partial(chunk_kernel, red_size, length, start, 1 if aliases else 0),
                n_in,
                len(deps),
            ),
            grid_spec=pltpu.PrefetchScalarGridSpec(
                num_scalar_prefetch=1,
                grid=(1,),
                in_specs=in_specs,
                out_specs=[ANY] * 8 + [whole((3 * half, width))],
                scratch_shapes=[
                    pltpu.VMEM((n_rows, model_width), jnp.bfloat16),
                    pltpu.VMEM((model_width, n_rows), jnp.bfloat16),
                    pltpu.VMEM((model_width, 2 * width), jnp.bfloat16),
                    pltpu.VMEM((model_width, 2 * width), jnp.bfloat16),
                    pltpu.VMEM((own_rows, width), jnp.bfloat16),
                    pltpu.VMEM((own_rows, width), jnp.bfloat16),
                    pltpu.VMEM((n_rows, 2 * width), jnp.bfloat16),
                    pltpu.SemaphoreType.DMA((3 * red_size - 1,)),
                    pltpu.SemaphoreType.DMA,
                    pltpu.SemaphoreType.DMA,
                    pltpu.SemaphoreType.DMA((4,)),
                    pltpu.SemaphoreType.DMA((4 * red_size,)),
                ],
            ),
            out_shape=[
                pltpu.HBM((own_rows, side), jnp.bfloat16),
                pltpu.HBM((own_rows, side), jnp.bfloat16),
                *[jax.ShapeDtypeStruct((red_size, part, 2 * width), jnp.bfloat16)] * 4,
                pltpu.HBM((n_rows, 2 * width), jnp.bfloat16),
                jax.ShapeDtypeStruct((model_width, 2 * width), jnp.bfloat16),
                jax.ShapeDtypeStruct((3 * half, width), jnp.float32),
            ],
            input_output_aliases=aliases,
            compiler_params=params(),
            cost_estimate=LONG,
        )(idx, *operands)

    def add_plane(parts, *deps):
        shape = parts[0].shape
        return pl.pallas_call(
            ordered(plane_kernel, 4, len(deps)),
            grid=(1,),
            in_specs=[whole(shape)] * 4 + [ANY] * len(deps),
            out_specs=whole(shape),
            out_shape=jax.ShapeDtypeStruct(shape, jnp.bfloat16),
            compiler_params=params(),
            cost_estimate=LONG,
        )(*parts, *deps)

    def send_plane(grads):
        return [grads[0], *(to_quarter(grads[r], r) for r in range(1, 4))]

    def send_line(parts):
        return lax.all_to_all(parts, "red", 0, 0, tiled=True)

    def add_line(parts, *deps):
        shape = parts[0].shape
        out_shape = (len(parts), *shape[1:])
        kind = jnp.bfloat16 if dp_size <= 8 else jnp.float32
        owned = pl.pallas_call(
            ordered(functools.partial(line_kernel, len(parts)), 1 + len(parts), len(deps)),
            grid=(1,),
            in_specs=[pl.BlockSpec(memory_space=pltpu.SMEM)]
            + [whole(shape)] * len(parts)
            + [ANY] * len(deps),
            out_specs=whole(out_shape),
            out_shape=jax.ShapeDtypeStruct(out_shape, kind),
            compiler_params=params(),
            cost_estimate=LONG,
        )(root.reshape(1), *parts, *deps)
        return other_groups(owned).astype(jnp.bfloat16)

    def spread(owned, *deps):
        parts = [owned, *(to_quarter(owned, r) for r in range(1, 4))]
        return pl.pallas_call(
            ordered(stack_kernel, 4, len(deps)),
            grid=(1,),
            in_specs=[whole(owned.shape)] * 4 + [ANY] * len(deps),
            out_specs=whole((4, *owned.shape)),
            out_shape=jax.ShapeDtypeStruct((4, *owned.shape), owned.dtype),
            compiler_params=params(),
            cost_estimate=SHORT,
        )(*parts, *deps)

    def place(first, mine, sib, grad_out, estimate):
        start, width = CHUNKS[first]
        near_column, columns = start // width, side // width
        has_out = 0 if grad_out is None else 1
        operands = [mine, sib] + ([grad_out] if has_out else [])
        return pl.pallas_call(
            functools.partial(place_kernel, has_out),
            grid_spec=pltpu.PrefetchScalarGridSpec(
                num_scalar_prefetch=1,
                grid=(mine.shape[1], 2, 2),
                in_specs=[whole(mine.shape)] * 2 + [ANY] * has_out,
                out_specs=pl.BlockSpec(
                    (block, width),
                    lambda k, c, h, idx: (0, near_column + k + c * columns + h * 2 * columns),
                ),
            ),
            out_shape=pltpu.HBM((block, 2 * model_width), jnp.float32),
            input_output_aliases={3: 0} if has_out else {},
            compiler_params=params(),
            cost_estimate=estimate,
        )(idx, *operands)

    outs, ghs, ws, sums = None, [], [], []
    on_way, planes, after_plane = [], [], []

    def step_plane(chunk, *deps):
        after_plane.append(add_plane(on_way[chunk], *deps))
        planes.append(send_line(after_plane[-1]))

    for chunk in range(n_chunks):
        deps = []
        if chunk == 0 and n_chunks > 1:
            deps += [packed[1][0], *firsts]
        if chunk + 1 < n_chunks and chunk > 0:
            packed.append(second_pack(z[chunk + 1], sums[-1]))
            near.append(second_sends(packed[-1]))
            deps += [packed[-1][0]]
        if chunk >= 2:
            step_plane(chunk - 2, sums[-1])
            deps += [after_plane[-1]]
        *outs, g0, g1, g2, g3, gh, w, tap_sums = middle(chunk, outs, deps)
        on_way.append(send_plane([g0, g1, g2, g3]))
        ghs.append(gh)
        ws.append(w)
        sums.append(tap_sums)

    out_other = to_core(outs[1])
    step = own_rows // 2
    steps = own_rows // step
    row_spec = pl.BlockSpec((step, model_width), lambda i, *_: (i, 0))
    gh_specs = [pl.BlockSpec((step, gh.shape[1]), lambda i, *_: (i, 0)) for gh in ghs]
    sib_specs = [pl.BlockSpec((step, gh.shape[1]), lambda i, *_: (i + steps, 0)) for gh in ghs]
    w_specs = [whole(w.shape) for w in ws]
    flops = 2 * own_rows * model_width * model_width
    deps = [sums[-1]]
    while len(planes) < n_chunks - 1:
        step_plane(len(planes), sums[-1])
        deps.append(after_plane[-1])
    grad_scaled_sib = pl.pallas_call(
        ordered(functools.partial(grad_scaled_kernel, n_chunks), 2 * n_chunks, len(deps)),
        grid=(1,),
        in_specs=[pl.BlockSpec((own_rows, gh.shape[1]), lambda i: (1, 0)) for gh in ghs]
        + w_specs
        + [ANY] * len(deps),
        out_specs=whole((own_rows, model_width)),
        out_shape=pltpu.HBM((own_rows, model_width), jnp.bfloat16),
        compiler_params=params(),
        cost_estimate=LONG,
    )(*ghs, *ws, *deps)
    other = to_core(grad_scaled_sib)
    early = add_line(planes, grad_scaled_sib)
    step_plane(n_chunks - 1, early)
    deps = [after_plane[-1]]
    side_spec = pl.BlockSpec((step, side), lambda i, *_: (i, 0))
    module_output, frame_gradient, gain_part = pl.pallas_call(
        ordered(functools.partial(frame_kernel, n_chunks), 8 + 2 * n_chunks, len(deps)),
        grid_spec=pltpu.PrefetchScalarGridSpec(
            num_scalar_prefetch=1,
            grid=(steps,),
            in_specs=[
                row_spec,
                row_spec,
                pl.BlockSpec((step, 128), lambda i, *_: (i, 0)),
                whole((1, model_width)),
                row_spec,
                side_spec,
                side_spec,
                *gh_specs,
                *w_specs,
                *[ANY] * len(deps),
            ],
            out_specs=[row_spec, row_spec, whole((8, model_width))],
        ),
        out_shape=[
            jax.ShapeDtypeStruct((own_rows, model_width), jnp.bfloat16),
            jax.ShapeDtypeStruct((own_rows, model_width), jnp.bfloat16),
            jax.ShapeDtypeStruct((8, model_width), jnp.float32),
        ],
        compiler_params=params(),
        cost_estimate=LONG,
    )(
        idx,
        flat_frames,
        flat_cot,
        live,
        gain.reshape(1, model_width),
        other,
        outs[0],
        out_other,
        *ghs,
        *ws,
        *deps,
    )

    mine = spread(early)
    grad_out = place(0, mine, to_core(mine), None, LONG)
    mine = spread(add_line(planes[-1:]), grad_out)
    grad_out = place(n_chunks - 1, mine, to_core(mine), grad_out, SHORT)

    order = sorted(range(n_chunks), key=lambda c: CHUNKS[c][0])
    tap_part = jnp.dot(
        back_matrix,
        jnp.concatenate([sums[c] for c in order], axis=1),
        precision=lax.Precision.HIGHEST,
    )
    gain_part = jnp.sum(gain_part, axis=0).reshape(2, side)
    small = jnp.concatenate([tap_part, gain_part], axis=0)
    for r in (1, 2):
        small = small + to_quarter(small, r)
    bit = 1
    while bit < red_size:
        small = small + lax.ppermute(small, "red", [(i, i ^ bit) for i in range(red_size)])
        bit *= 2
    small = other_groups(small) * root
    both = to_core(small)
    first = core == 0
    left, right = jnp.where(first, small, both), jnp.where(first, both, small)
    tap_total = jnp.concatenate([left[:taps], right[:taps]], axis=1)
    gain_total = (small[taps:] + both[taps:]).reshape(model_width)
    return (
        module_output.reshape(frames.shape),
        frame_gradient.reshape(frames.shape),
        grad_out,
        tap_total,
        gain_total,
    )


def solution(mesh):
    placed = (
        P(("dp", "red"), None, None),
        P(("dp", "red"), None, None),
        P("red", None),
        P(),
        P(),
        P(),
    )
    return jax.shard_map(
        local,
        mesh=mesh,
        in_specs=placed,
        out_specs=(
            P(("dp", "red"), None, None),
            P(("dp", "red"), None, None),
            P("red", None),
            P(),
            P(),
        ),
        check_vma=False,
    )
```
